32 devices in a mesh: rows: 8 (over z, x), cols: 4 (over y, core).
Axes of the slice: x: 2, y: 2, z: 4, core: 2. Of those that a mesh axis runs over, the one named last changes fastest.
Arguments:
- matrix: bfloat16 [16384, 1024], P('rows', 'cols'), as said below
- row_signs: int32 [16384], P('rows'), may hold values from 0 to 1
- sampled_rows: int32 [8, 2048], P('rows'), may hold values from 0 to 2047
- right_sides: float32 [8, 16384], P(None, 'rows'), may hold values from -6 to 6
Outputs:
- solution: float32 [8, 1024], P(None, 'cols')
- residual: float32 [8, 16384], P(None, 'rows')
The draws below stay inside these ranges and needn't reach their ends.
Inputs may be any that keep to these rules, and one draw needn't show every extreme that they name: `matrix`: entries are at most 70 / sqrt(16384) in magnitude.
All inputs are finite; a program needn't handle non-finite values.
Results may differ from the reference program's by a relative error of at most 0.0013.
Values sent between devices are 32-bit elements; how exact they have to be, the bound alone decides.
A program may use at most 64 MiB of HBM per device.

```python
import math
import jax
import jax.numpy as jnp
from jax import lax

UNKNOWNS = 1024
SKETCH = 2048
SYSTEMS = 8
ROUNDS = 2
BLOCK_ROWS = 2048
BLOCKS = 8
EQUATIONS = 16384


def column_mixer(mix_key):
    square = jax.random.normal(mix_key, (UNKNOWNS, UNKNOWNS), jnp.float32)
    basis, _ = jnp.linalg.qr(square)
    ladder = jnp.exp(jnp.linspace(0.0, math.log(30.0), UNKNOWNS).astype(jnp.float32))
    ladder = ladder / jnp.sqrt(jnp.mean(ladder * ladder))
    return jnp.dot(basis * ladder[None, :], basis.T)


def draw_matrix(key, part):
    noise_key = jax.random.fold_in(jax.random.fold_in(key, 17), 0)
    scale_key = jax.random.fold_in(jax.random.fold_in(key, 17), 1)
    mix_key = jax.random.fold_in(jax.random.fold_in(key, 17), 3)
    scales = jnp.exp(jax.random.uniform(scale_key, (BLOCKS, 1, UNKNOWNS), jnp.float32) * math.log(10.0))
    base = jnp.clip(jax.random.normal(noise_key, (BLOCKS, BLOCK_ROWS, UNKNOWNS), jnp.float32), -4.0, 4.0)
    scaled = (base * scales).reshape(EQUATIONS, UNKNOWNS)
    mixed = jnp.dot(scaled, column_mixer(mix_key))
    result = jnp.clip(mixed, -60.0, 60.0) / math.sqrt(EQUATIONS)
    return result.astype(jnp.bfloat16)


def with_ends(array, rng, smallest, top_value):
    place = [jax.random.randint(jax.random.fold_in(rng, axis), (), 0, length) for axis, length in enumerate(array.shape)]
    longest = array.shape.index(max(array.shape))
    next_to = place[:longest] + [(place[longest] + 1) % array.shape[longest]] + place[longest + 1:]
    return array.at[tuple(place)].set(smallest).at[tuple(next_to)].set(top_value)


def shard_levels(stream_key, dims, shards, low, top_value):
    def one(position, blocks):
        draws = jax.random.uniform(jax.random.fold_in(jax.random.fold_in(stream_key, 6), position), (blocks,), jnp.float32, low / len(shards), top_value / len(shards))
        return jnp.repeat(jnp.exp(draws), dims[position] // blocks).reshape((-1,) + (1,) * (len(dims) - position - 1))

    level = one(*shards[0])
    for cut in shards[1:]:
        level = level * one(*cut)
    return level


def scatter_about(key, dims, spread, bound, cuts=(), kind=jnp.bfloat16):
    factor_of = shard_levels(key, dims, cuts, -0.22, 0.18) if cuts else 1.0
    values = jax.random.normal(key, dims, jnp.float32) * spread * factor_of
    return jnp.minimum(jnp.maximum(values, -bound), bound).astype(kind)


def setup_inputs(seed: int = 0) -> dict:
    splits = jax.random.split(jax.random.key(seed), 5)
    return {
        "matrix": draw_matrix(jax.random.fold_in(splits[4], 71), 0),
        "row_signs": with_ends(jax.random.randint(splits[1], (EQUATIONS,), 0, 2), jax.random.fold_in(splits[1], 1), 0, 1).astype(jnp.int32),
        "sampled_rows": with_ends(jax.random.randint(splits[2], (BLOCKS, SKETCH), 0, BLOCK_ROWS), jax.random.fold_in(splits[2], 1), 0, BLOCK_ROWS - 1).astype(jnp.int32),
        "right_sides": scatter_about(splits[3], (SYSTEMS, EQUATIONS), 1.0, 6.0, ((1, 8),), jnp.float32),
    }


highest = lax.Precision.HIGHEST

def sylvester(matrix_order):
    positions = jnp.arange(matrix_order, dtype=jnp.int32)
    common = jnp.bitwise_and(positions[:, None], positions[None, :])
    parity = jnp.zeros((matrix_order, matrix_order), jnp.int32)
    for bit_place in range(max(matrix_order.bit_length() - 1, 0)):
        parity = parity + jnp.bitwise_and(jnp.right_shift(common, bit_place), 1)
    return jnp.where(jnp.bitwise_and(parity, 1) == 0, 1.0, -1.0).astype(jnp.float32)

def hadamard(signed):
    row_count, col_count = signed.shape
    bit_count = row_count.bit_length() - 1
    factor_sizes = []
    while bit_count > 0:
        group_bits = min(4, bit_count)
        factor_sizes.append(2 ** group_bits)
        bit_count = bit_count - group_bits
    result = signed
    for factor_size in factor_sizes:
        shaped = result.reshape(factor_size, row_count // factor_size, col_count)
        result = jnp.einsum('ab,bmn->man', sylvester(factor_size), shaped, precision=highest).reshape(row_count, col_count)
    return result

def solve_right(factor, vectors):
    return lax.linalg.triangular_solve(factor, vectors, left_side=False, lower=True, transpose_a=True)

def solve_left(factor, vectors):
    return lax.linalg.triangular_solve(factor, vectors, left_side=False, lower=True, transpose_a=False)

def reference(matrix, row_signs, sampled_rows, right_sides):
    row_blocks = matrix.reshape(BLOCKS, BLOCK_ROWS, UNKNOWNS)
    sign_blocks = (1 - 2 * row_signs).reshape(BLOCKS, BLOCK_ROWS)
    systems = right_sides.shape[0]

    def sketch_step(running, scan_item):
        row_block, sign_column, sample_row = scan_item
        signed = row_block.astype(jnp.float32) * sign_column.astype(jnp.float32)[:, None]
        mixed_rows = hadamard(signed)
        picked = jnp.take(mixed_rows, sample_row, axis=0) * (1.0 / math.sqrt(SKETCH))
        return (running + picked, None)
    sketch, _ = lax.scan(sketch_step, jnp.zeros((SKETCH, UNKNOWNS), jnp.float32), (row_blocks, sign_blocks, sampled_rows))
    gram_matrix = jnp.dot(sketch.T, sketch, precision=highest)
    factor = jnp.linalg.cholesky(gram_matrix)

    def forward(vectors):

        def one_block(row_block):
            return lax.dot_general(vectors, row_block.astype(jnp.float32), (((1,), (1,)), ((), ())), precision=highest)
        pieces = lax.map(one_block, row_blocks)
        return jnp.transpose(pieces, (1, 0, 2)).reshape(systems, EQUATIONS)

    def backward(vectors):
        split = jnp.transpose(vectors.reshape(systems, BLOCKS, BLOCK_ROWS), (1, 0, 2))

        def add_block(running, scan_item):
            row_block, part_rows = scan_item
            return (running + jnp.dot(part_rows, row_block.astype(jnp.float32), precision=highest), None)
        summed, _ = lax.scan(add_block, jnp.zeros((systems, UNKNOWNS), jnp.float32), (row_blocks, split))
        return summed
    beta_norm = jnp.sqrt(lax.optimization_barrier(jnp.sum(right_sides * right_sides, axis=1)))
    left_unit = right_sides / beta_norm[:, None]
    back_rest = solve_right(factor, backward(left_unit))
    alpha_norm = jnp.sqrt(lax.optimization_barrier(jnp.sum(back_rest * back_rest, axis=1)))
    right_unit = back_rest / alpha_norm[:, None]
    search = right_unit
    coeffs = jnp.zeros((systems, UNKNOWNS), jnp.float32)
    phibar = beta_norm
    rhobar = alpha_norm
    for iteration in range(ROUNDS):
        forward_rest = forward(solve_left(factor, right_unit)) - alpha_norm[:, None] * left_unit
        beta_norm = jnp.sqrt(lax.optimization_barrier(jnp.sum(forward_rest * forward_rest, axis=1)))
        left_unit = forward_rest / beta_norm[:, None]
        back_rest = solve_right(factor, backward(left_unit)) - beta_norm[:, None] * right_unit
        alpha_norm = jnp.sqrt(lax.optimization_barrier(jnp.sum(back_rest * back_rest, axis=1)))
        right_unit = back_rest / alpha_norm[:, None]
        rho_total = jnp.sqrt(rhobar * rhobar + beta_norm * beta_norm)
        cosine = rhobar / rho_total
        sine_part = beta_norm / rho_total
        theta_term = sine_part * alpha_norm
        rhobar = -cosine * alpha_norm
        phi_term = cosine * phibar
        phibar = sine_part * phibar
        coeffs = coeffs + (phi_term / rho_total)[:, None] * search
        search = right_unit - (theta_term / rho_total)[:, None] * search
    solution = solve_left(factor, coeffs)
    residual = right_sides - forward(solution)
    return (solution, residual)
```

```python
import functools
import math

import jax
import jax.numpy as jnp
from jax import lax
from jax.experimental import pallas as pl
from jax.experimental.pallas import tpu as pltpu
from jax.sharding import PartitionSpec as P

ROUNDS = 2
BLOCK = 128
STRIP = 8

highest = lax.Precision.HIGHEST


def sylvester(matrix_order):
    positions = jnp.arange(matrix_order, dtype=jnp.int32)
    common = jnp.bitwise_and(positions[:, None], positions[None, :])
    parity = jnp.zeros((matrix_order, matrix_order), jnp.int32)
    for bit_place in range(max(matrix_order.bit_length() - 1, 0)):
        parity = parity + jnp.bitwise_and(jnp.right_shift(common, bit_place), 1)
    return jnp.where(jnp.bitwise_and(parity, 1) == 0, 1.0, -1.0).astype(jnp.float32)


def block_inverse(square):
    size = square.shape[0]
    row_ids = lax.broadcasted_iota(jnp.int32, (size, size), 0)
    col_ids = lax.broadcasted_iota(jnp.int32, (size, size), 1)
    rest = square
    unit = jnp.where(row_ids == col_ids, 1.0, 0.0).astype(jnp.float32)
    finished = []
    for strip in range(size // STRIP):
        start = strip * STRIP
        height = size - start
        here = lax.broadcasted_iota(jnp.int32, (height, size), 0)
        columns = [
            jnp.broadcast_to(rest[:, start + k:start + k + 1], (height, size)) for k in range(STRIP)
        ]
        scale = jnp.ones((STRIP, size), jnp.float32)
        for k in range(STRIP):
            pivot = columns[k][k:k + 1, :]
            factors = jnp.where(here > k, columns[k] * (1.0 / pivot), 0.0)
            for later in range(k + 1, STRIP):
                columns[later] = columns[later] - factors * columns[later][k:k + 1, :]
            rest = rest - factors * rest[k:k + 1, :]
            unit = unit - factors * unit[k:k + 1, :]
            scale = jnp.where(here[:STRIP] == k, lax.rsqrt(pivot), scale)
        finished.append(unit[:STRIP] * scale)
        rest = rest[STRIP:]
        unit = unit[STRIP:]
    return jnp.concatenate(finished, axis=0)


def inverse_factor_kernel(gram_ref, out_ref, strip_ref):
    order = gram_ref.shape[0]
    blocks = order // BLOCK
    out_ref[...] = gram_ref[...]

    def step(block, carry):
        start = pl.multiple_of(block * BLOCK, BLOCK)
        own = pl.ds(start, BLOCK)
        inverse = block_inverse(out_ref[own, own])
        strip_ref[...] = jnp.dot(
            inverse, out_ref[own, :], precision=highest, preferred_element_type=jnp.float32
        )
        strip_ref[:, own] = inverse

        def update(row_block, inner):
            rows = pl.ds(pl.multiple_of(row_block * BLOCK, BLOCK), BLOCK)
            out_ref[rows, own] = jnp.zeros((BLOCK, BLOCK), jnp.float32)
            out_ref[rows, :] = out_ref[rows, :] - lax.dot_general(
                strip_ref[:, rows], strip_ref[...], (((0,), (0,)), ((), ())),
                precision=highest, preferred_element_type=jnp.float32,
            )
            return inner

        lax.fori_loop(block + 1, blocks, update, 0)
        col_ids = lax.broadcasted_iota(jnp.int32, (BLOCK, order), 1)
        out_ref[own, :] = jnp.where(col_ids < start + BLOCK, strip_ref[...], 0.0)
        return carry

    lax.fori_loop(0, blocks, step, 0)


def inverse_factor(gram_matrix):
    order = gram_matrix.shape[0]
    return pl.pallas_call(
        inverse_factor_kernel,
        out_shape=jax.ShapeDtypeStruct((order, order), jnp.float32),
        in_specs=[pl.BlockSpec(memory_space=pltpu.VMEM)],
        out_specs=pl.BlockSpec(memory_space=pltpu.VMEM),
        scratch_shapes=[pltpu.VMEM((BLOCK, order), jnp.float32)],
        compiler_params=pltpu.CompilerParams(vmem_limit_bytes=32 * 1024 * 1024),
    )(gram_matrix)


def picked_mixer(sampled, row_count):
    bit_count = row_count.bit_length() - 1
    inner_order = 2 ** (bit_count // 2)
    outer_order = row_count // inner_order
    outer = jnp.take(sylvester(outer_order).astype(jnp.bfloat16), sampled // inner_order, axis=0)
    inner = jnp.take(sylvester(inner_order).astype(jnp.bfloat16), sampled % inner_order, axis=0)
    return (outer[:, :, None] * inner[:, None, :]).reshape(sampled.shape[0], row_count)


def local(matrix, row_signs, sampled_rows, right_sides):
    row_count, col_count = matrix.shape
    flipped = (1 - 2 * row_signs).astype(jnp.bfloat16)
    signed = matrix * flipped[:, None]
    picked = jnp.dot(
        picked_mixer(sampled_rows[0], row_count), signed, preferred_element_type=jnp.float32
    ) * (1.0 / math.sqrt(sampled_rows.shape[1]))
    sketch_piece = lax.psum_scatter(picked, "rows", scatter_dimension=0, tiled=True)
    gram_block = lax.dot_general(
        lax.all_gather(sketch_piece, "cols", axis=1, tiled=True),
        sketch_piece,
        (((0,), (0,)), ((), ())),
        precision=highest,
    )
    gram_summed = lax.psum(gram_block, "rows")
    gram_matrix = lax.all_gather(gram_summed, "cols", axis=1, tiled=True)
    inverse = inverse_factor(gram_matrix)
    col_start = lax.axis_index("cols") * col_count
    wide = matrix.astype(jnp.float32)

    def forward(vectors):
        own_part = lax.dynamic_slice_in_dim(vectors, col_start, col_count, 1)
        local_part = lax.dot_general(own_part, wide, (((1,), (1,)), ((), ())), precision=highest)
        return lax.psum(local_part, "cols")

    def backward(vectors):
        squares = jnp.sum(vectors * vectors, axis=1)
        local_part = jnp.dot(vectors, wide, precision=highest)
        summed, total = lax.psum((local_part, squares), "rows")
        return jnp.sqrt(total), lax.all_gather(summed, "cols", axis=1, tiled=True)

    def solve_right(vectors):
        return lax.dot_general(vectors, inverse, (((1,), (1,)), ((), ())), precision=highest)

    def solve_left(vectors):
        return jnp.dot(vectors, inverse, precision=highest)

    beta_norm, whole_vector = backward(right_sides)
    left_unit = right_sides / beta_norm[:, None]
    back_rest = solve_right(whole_vector / beta_norm[:, None])
    alpha_norm = jnp.sqrt(jnp.sum(back_rest * back_rest, axis=1))
    right_unit = back_rest / alpha_norm[:, None]
    moved = solve_left(right_unit)
    image = forward(moved)
    search, search_image = moved, image
    full_solution = jnp.zeros_like(moved)
    solution_image = jnp.zeros_like(image)
    phibar = beta_norm
    rhobar = alpha_norm
    for iteration in range(ROUNDS):
        forward_rest = image - alpha_norm[:, None] * left_unit
        if iteration < ROUNDS - 1:
            beta_norm, whole_vector = backward(forward_rest)
        else:
            beta_norm = jnp.sqrt(lax.psum(jnp.sum(forward_rest * forward_rest, axis=1), "rows"))
        rho_total = jnp.sqrt(rhobar * rhobar + beta_norm * beta_norm)
        cosine = rhobar / rho_total
        sine_part = beta_norm / rho_total
        phi_term = cosine * phibar
        ratio = (phi_term / rho_total)[:, None]
        full_solution = full_solution + ratio * search
        solution_image = solution_image + ratio * search_image
        if iteration == ROUNDS - 1:
            break
        left_unit = forward_rest / beta_norm[:, None]
        back_rest = solve_right(whole_vector / beta_norm[:, None]) - beta_norm[:, None] * right_unit
        alpha_norm = jnp.sqrt(jnp.sum(back_rest * back_rest, axis=1))
        right_unit = back_rest / alpha_norm[:, None]
        moved = solve_left(right_unit)
        image = forward(moved)
        theta_term = sine_part * alpha_norm
        rhobar = -cosine * alpha_norm
        phibar = sine_part * phibar
        shrink = (theta_term / rho_total)[:, None]
        search = moved - shrink * search
        search_image = image - shrink * search_image
    residual = right_sides - solution_image
    solution = lax.dynamic_slice_in_dim(full_solution, col_start, col_count, 1)
    return (solution, residual)


def solution(mesh):
    in_specs = (P("rows", "cols"), P("rows"), P("rows", None), P(None, "rows"))
    out_specs = (P(None, "cols"), P(None, "rows"))
    return jax.shard_map(local, mesh=mesh, in_specs=in_specs, out_specs=out_specs, check_vma=False)
```

```python
import functools
import math

import jax
import jax.numpy as jnp
from jax import lax
from jax.experimental import pallas as pl
from jax.experimental.pallas import tpu as pltpu
from jax.sharding import PartitionSpec as P

ROUNDS = 2
BLOCK = 128
STRIP = 8

highest = lax.Precision.HIGHEST


def sylvester(matrix_order):
    positions = jnp.arange(matrix_order, dtype=jnp.int32)
    common = jnp.bitwise_and(positions[:, None], positions[None, :])
    parity = jnp.zeros((matrix_order, matrix_order), jnp.int32)
    for bit_place in range(max(matrix_order.bit_length() - 1, 0)):
        parity = parity + jnp.bitwise_and(jnp.right_shift(common, bit_place), 1)
    return jnp.where(jnp.bitwise_and(parity, 1) == 0, 1.0, -1.0).astype(jnp.float32)


def block_inverse(square):
    size = square.shape[0]
    row_ids = lax.broadcasted_iota(jnp.int32, (size, size), 0)
    col_ids = lax.broadcasted_iota(jnp.int32, (size, size), 1)
    rest = square
    unit = jnp.where(row_ids == col_ids, 1.0, 0.0).astype(jnp.float32)
    finished = []
    for strip in range(size // STRIP):
        start = strip * STRIP
        height = size - start
        here = lax.broadcasted_iota(jnp.int32, (height, size), 0)
        columns = [
            jnp.broadcast_to(rest[:, start + k:start + k + 1], (height, size)) for k in range(STRIP)
        ]
        scale = jnp.ones((STRIP, size), jnp.float32)
        for k in range(STRIP):
            pivot = columns[k][k:k + 1, :]
            factors = jnp.where(here > k, columns[k] * (1.0 / pivot), 0.0)
            for later in range(k + 1, STRIP):
                columns[later] = columns[later] - factors * columns[later][k:k + 1, :]
            rest = rest - factors * rest[k:k + 1, :]
            unit = unit - factors * unit[k:k + 1, :]
            scale = jnp.where(here[:STRIP] == k, lax.rsqrt(pivot), scale)
        finished.append(unit[:STRIP] * scale)
        rest = rest[STRIP:]
        unit = unit[STRIP:]
    return jnp.concatenate(finished, axis=0)


def inverse_factor_kernel(gram_ref, out_ref, strip_ref):
    order = gram_ref.shape[0]
    blocks = order // BLOCK
    out_ref[...] = gram_ref[...]

    def step(block, carry):
        start = pl.multiple_of(block * BLOCK, BLOCK)
        own = pl.ds(start, BLOCK)
        inverse = block_inverse(out_ref[own, own])
        strip_ref[...] = jnp.dot(
            inverse, out_ref[own, :], precision=highest, preferred_element_type=jnp.float32
        )
        strip_ref[:, own] = inverse

        def update(row_block, inner):
            rows = pl.ds(pl.multiple_of(row_block * BLOCK, BLOCK), BLOCK)
            out_ref[rows, own] = jnp.zeros((BLOCK, BLOCK), jnp.float32)
            out_ref[rows, :] = out_ref[rows, :] - lax.dot_general(
                strip_ref[:, rows], strip_ref[...], (((0,), (0,)), ((), ())),
                precision=highest, preferred_element_type=jnp.float32,
            )
            return inner

        lax.fori_loop(block + 1, blocks, update, 0)
        col_ids = lax.broadcasted_iota(jnp.int32, (BLOCK, order), 1)
        out_ref[own, :] = jnp.where(col_ids < start + BLOCK, strip_ref[...], 0.0)
        return carry

    lax.fori_loop(0, blocks, step, 0)


def inverse_factor(gram_matrix):
    order = gram_matrix.shape[0]
    return pl.pallas_call(
        inverse_factor_kernel,
        out_shape=jax.ShapeDtypeStruct((order, order), jnp.float32),
        in_specs=[pl.BlockSpec(memory_space=pltpu.VMEM)],
        out_specs=pl.BlockSpec(memory_space=pltpu.VMEM),
        scratch_shapes=[pltpu.VMEM((BLOCK, order), jnp.float32)],
        compiler_params=pltpu.CompilerParams(vmem_limit_bytes=32 * 1024 * 1024),
    )(gram_matrix)


MESH = pl.DeviceIdType.MESH


def greet(axes):
    barrier = pltpu.get_barrier_semaphore()
    count = 0
    for axis in axes:
        size = lax.axis_size(axis)
        me = lax.axis_index(axis)
        for offset in range(1, size):
            pl.semaphore_signal(
                barrier, inc=1, device_id={axis: lax.rem(me + offset, size)}, device_id_type=MESH
            )
        count += size - 1
    pl.semaphore_wait(barrier, count)


def share(axis, value, slots, send_sem, recv_sem):
    size = lax.axis_size(axis)
    me = lax.axis_index(axis)
    slots[me] = value

    def copy(slot, offset, peer):
        return pltpu.make_async_remote_copy(
            src_ref=slots.at[slot], dst_ref=slots.at[slot],
            send_sem=send_sem.at[offset - 1], recv_sem=recv_sem.at[slot],
            device_id={axis: peer}, device_id_type=MESH,
        )

    for offset in range(1, size):
        copy(me, offset, lax.rem(me + offset, size)).start()
    for offset in range(1, size):
        source = lax.rem(me + size - offset, size)
        copy(source, offset, source).wait_recv()
    for offset in range(1, size):
        copy(me, offset, lax.rem(me + offset, size)).wait_send()


def split_rows(vectors):
    top = vectors.astype(jnp.bfloat16).astype(jnp.float32)
    rest = vectors - top
    middle = rest.astype(jnp.bfloat16).astype(jnp.float32)
    low = rest - middle
    return jnp.concatenate([top, middle, low, jnp.zeros_like(low)], axis=0).astype(jnp.bfloat16)


def join_rows(stacked, systems):
    return stacked[:systems] + stacked[systems:2 * systems] + stacked[2 * systems:3 * systems]


def lsqr_kernel(
    matrix_ref, inverse_ref, right_ref, solution_ref, residual_ref,
    row_slots, col_slots, image_slots, norm_slots,
    row_send, row_recv, col_send, col_recv, image_send, image_recv, norm_send, norm_recv,
):
    systems = right_ref.shape[0]
    col_count = matrix_ref.shape[1]
    own = pl.ds(pl.multiple_of(lax.axis_index("cols") * col_count, col_count), col_count)
    greet(("rows", "cols"))

    def added(slots):
        total = slots[0]
        for slot in range(1, slots.shape[0]):
            total = total + slots[slot]
        return total

    def forward(own_part, turn):
        product = lax.dot_general(
            split_rows(own_part), matrix_ref[...], (((1,), (1,)), ((), ())),
            preferred_element_type=jnp.float32,
        )
        share("cols", join_rows(product, systems), image_slots.at[turn], image_send.at[turn], image_recv.at[turn])
        return added(image_slots.at[turn])

    def backward(vectors, turn):
        squares = jnp.sum(vectors * vectors, axis=1, keepdims=True)
        product = jnp.dot(split_rows(vectors), matrix_ref[...], preferred_element_type=jnp.float32)
        value = jnp.concatenate(
            [join_rows(product, systems), jnp.broadcast_to(squares, (systems, col_count))], axis=0
        )
        share("rows", value, row_slots.at[turn], row_send.at[turn], row_recv.at[turn])
        total = added(row_slots.at[turn])
        norm = jnp.sqrt(total[systems:, 0:1])
        share("cols", total[:systems] / norm, col_slots.at[turn], col_send.at[turn], col_recv.at[turn])
        whole = jnp.concatenate([col_slots[turn, slot] for slot in range(col_slots.shape[1])], axis=1)
        return norm, whole

    def solve_right(vectors):
        return lax.dot_general(
            vectors, inverse_ref[...], (((1,), (1,)), ((), ())),
            precision=highest, preferred_element_type=jnp.float32,
        )

    def solve_left(vectors):
        return jnp.dot(vectors, inverse_ref[:, own], precision=highest, preferred_element_type=jnp.float32)

    def norm_of(vectors):
        return jnp.sqrt(jnp.sum(vectors * vectors, axis=1, keepdims=True))

    right_sides = right_ref[...]
    beta_norm, whole_vector = backward(right_sides, 0)
    left_unit = right_sides / beta_norm
    back_rest = solve_right(whole_vector)
    alpha_norm = norm_of(back_rest)
    right_unit = back_rest / alpha_norm
    moved = solve_left(right_unit)
    image = forward(moved, 0)
    search, search_image = moved, image
    coeffs = jnp.zeros_like(moved)
    coeffs_image = jnp.zeros_like(image)
    phibar = beta_norm
    rhobar = alpha_norm
    for iteration in range(ROUNDS):
        last = iteration == ROUNDS - 1
        forward_rest = image - alpha_norm * left_unit
        if last:
            squares = jnp.sum(forward_rest * forward_rest, axis=1, keepdims=True)
            share("rows", jnp.broadcast_to(squares, norm_slots.shape[1:]), norm_slots, norm_send, norm_recv)
            beta_norm = jnp.sqrt(added(norm_slots)[:, 0:1])
        else:
            beta_norm, whole_vector = backward(forward_rest, iteration + 1)
        rho_total = jnp.sqrt(rhobar * rhobar + beta_norm * beta_norm)
        cosine = rhobar / rho_total
        sine_part = beta_norm / rho_total
        ratio = cosine * phibar / rho_total
        coeffs = coeffs + ratio * search
        coeffs_image = coeffs_image + ratio * search_image
        if last:
            break
        left_unit = forward_rest / beta_norm
        back_rest = solve_right(whole_vector) - beta_norm * right_unit
        alpha_norm = norm_of(back_rest)
        right_unit = back_rest / alpha_norm
        moved = solve_left(right_unit)
        image = forward(moved, iteration + 1)
        shrink = sine_part * alpha_norm / rho_total
        rhobar = -cosine * alpha_norm
        phibar = sine_part * phibar
        search = moved - shrink * search
        search_image = image - shrink * search_image
    solution_ref[...] = coeffs
    residual_ref[...] = right_sides - coeffs_image


def lsqr(matrix, inverse, right_sides):
    row_count, col_count = matrix.shape
    systems = right_sides.shape[0]
    row_size, col_size = lax.axis_size("rows"), lax.axis_size("cols")
    vmem = pl.BlockSpec(memory_space=pltpu.VMEM)
    dma = pltpu.SemaphoreType.DMA
    return pl.pallas_call(
        lsqr_kernel,
        out_shape=(
            jax.ShapeDtypeStruct((systems, col_count), jnp.float32),
            jax.ShapeDtypeStruct((systems, row_count), jnp.float32),
        ),
        in_specs=[vmem] * 3,
        out_specs=(vmem, vmem),
        scratch_shapes=[
            pltpu.VMEM((ROUNDS, row_size, 2 * systems, col_count), jnp.float32),
            pltpu.VMEM((ROUNDS, col_size, systems, col_count), jnp.float32),
            pltpu.VMEM((ROUNDS, col_size, systems, row_count), jnp.float32),
            pltpu.VMEM((row_size, systems, 128), jnp.float32),
            dma((ROUNDS, row_size)), dma((ROUNDS, row_size)),
            dma((ROUNDS, col_size)), dma((ROUNDS, col_size)),
            dma((ROUNDS, col_size)), dma((ROUNDS, col_size)),
            dma((row_size,)), dma((row_size,)),
        ],
        compiler_params=pltpu.CompilerParams(
            collective_id=0, has_side_effects=True, vmem_limit_bytes=40 * 1024 * 1024
        ),
    )(matrix, inverse, right_sides)


def picked_mixer(sampled, row_count):
    bit_count = row_count.bit_length() - 1
    inner_order = 2 ** (bit_count // 2)
    outer_order = row_count // inner_order
    outer = jnp.take(sylvester(outer_order).astype(jnp.bfloat16), sampled // inner_order, axis=0)
    inner = jnp.take(sylvester(inner_order).astype(jnp.bfloat16), sampled % inner_order, axis=0)
    return (outer[:, :, None] * inner[:, None, :]).reshape(sampled.shape[0], row_count)


def local(matrix, row_signs, sampled_rows, right_sides):
    row_count, col_count = matrix.shape
    flipped = (1 - 2 * row_signs).astype(jnp.bfloat16)
    signed = matrix * flipped[:, None]
    picked = jnp.dot(
        picked_mixer(sampled_rows[0], row_count), signed, preferred_element_type=jnp.float32
    ) * (1.0 / math.sqrt(sampled_rows.shape[1]))
    sketch_piece = lax.psum_scatter(picked, "rows", scatter_dimension=0, tiled=True)
    gram_block = lax.dot_general(
        lax.all_gather(sketch_piece, "cols", axis=1, tiled=True),
        sketch_piece,
        (((0,), (0,)), ((), ())),
        precision=highest,
    )
    gram_summed = lax.psum(gram_block, "rows")
    gram_matrix = lax.all_gather(gram_summed, "cols", axis=1, tiled=True)
    inverse = inverse_factor(gram_matrix)
    return lsqr(matrix, inverse, right_sides)


def solution(mesh):
    in_specs = (P("rows", "cols"), P("rows"), P("rows", None), P(None, "rows"))
    out_specs = (P(None, "cols"), P(None, "rows"))
    return jax.shard_map(local, mesh=mesh, in_specs=in_specs, out_specs=out_specs, check_vma=False)
```

```python
import functools
import math

import jax
import jax.numpy as jnp
from jax import lax
from jax.experimental import pallas as pl
from jax.experimental.pallas import tpu as pltpu
from jax.sharding import PartitionSpec as P

ROUNDS = 2
BLOCK = 128
STRIP = 8

highest = lax.Precision.HIGHEST


def block_inverse(square):
    size = square.shape[0]
    row_ids = lax.broadcasted_iota(jnp.int32, (size, size), 0)
    col_ids = lax.broadcasted_iota(jnp.int32, (size, size), 1)
    rest = square
    unit = jnp.where(row_ids == col_ids, 1.0, 0.0).astype(jnp.float32)
    finished = []
    for strip in range(size // STRIP):
        start = strip * STRIP
        height = size - start
        here = lax.broadcasted_iota(jnp.int32, (height, size), 0)
        columns = [
            jnp.broadcast_to(rest[:, start + k:start + k + 1], (height, size)) for k in range(STRIP)
        ]
        scale = jnp.ones((STRIP, size), jnp.float32)
        for k in range(STRIP):
            pivot = columns[k][k:k + 1, :]
            factors = jnp.where(here > k, columns[k] * (1.0 / pivot), 0.0)
            for later in range(k + 1, STRIP):
                columns[later] = columns[later] - factors * columns[later][k:k + 1, :]
            rest = rest - factors * rest[k:k + 1, :]
            unit = unit - factors * unit[k:k + 1, :]
            scale = jnp.where(here[:STRIP] == k, lax.rsqrt(pivot), scale)
        finished.append(unit[:STRIP] * scale)
        rest = rest[STRIP:]
        unit = unit[STRIP:]
    return jnp.concatenate(finished, axis=0)


def inverse_factor_kernel(gram_ref, out_ref, strip_ref):
    order = gram_ref.shape[1]
    blocks = order // BLOCK
    width = gram_ref.shape[2]
    for col_block in range(gram_ref.shape[0]):
        out_ref[:, col_block * width:(col_block + 1) * width] = gram_ref[col_block]

    def step(block, carry):
        start = pl.multiple_of(block * BLOCK, BLOCK)
        own = pl.ds(start, BLOCK)
        inverse = block_inverse(out_ref[own, own])
        strip_ref[...] = jnp.dot(
            inverse, out_ref[own, :], precision=highest, preferred_element_type=jnp.float32
        )
        strip_ref[:, own] = inverse

        def update(row_block, inner):
            rows = pl.ds(pl.multiple_of(row_block * BLOCK, BLOCK), BLOCK)
            out_ref[rows, own] = jnp.zeros((BLOCK, BLOCK), jnp.float32)
            out_ref[rows, :] = out_ref[rows, :] - lax.dot_general(
                strip_ref[:, rows], strip_ref[...], (((0,), (0,)), ((), ())),
                precision=highest, preferred_element_type=jnp.float32,
            )
            return inner

        lax.fori_loop(block + 1, blocks, update, 0)
        col_ids = lax.broadcasted_iota(jnp.int32, (BLOCK, order), 1)
        out_ref[own, :] = jnp.where(col_ids < start + BLOCK, strip_ref[...], 0.0)
        return carry

    lax.fori_loop(0, blocks, step, 0)


def inverse_factor(gram_matrix):
    order = gram_matrix.shape[1]
    return pl.pallas_call(
        inverse_factor_kernel,
        out_shape=jax.ShapeDtypeStruct((order, order), jnp.float32),
        in_specs=[pl.BlockSpec(memory_space=pltpu.VMEM)],
        out_specs=pl.BlockSpec(memory_space=pltpu.VMEM),
        scratch_shapes=[pltpu.VMEM((BLOCK, order), jnp.float32)],
        compiler_params=pltpu.CompilerParams(vmem_limit_bytes=32 * 1024 * 1024),
    )(gram_matrix)


MESH = pl.DeviceIdType.MESH


def greet(axes):
    barrier = pltpu.get_barrier_semaphore()
    count = 0
    for axis in axes:
        size = lax.axis_size(axis)
        me = lax.axis_index(axis)
        for offset in range(1, size):
            pl.semaphore_signal(
                barrier, inc=1, device_id={axis: lax.rem(me + offset, size)}, device_id_type=MESH
            )
        count += size - 1
    pl.semaphore_wait(barrier, count)


def share_copy(axis, slots, send_sem, recv_sem, offset, incoming):
    size = lax.axis_size(axis)
    me = lax.axis_index(axis)
    peer = lax.rem(me + (size - offset if incoming else offset), size)
    slot = peer if incoming else me
    return pltpu.make_async_remote_copy(
        src_ref=slots.at[slot], dst_ref=slots.at[slot],
        send_sem=send_sem.at[offset - 1], recv_sem=recv_sem.at[slot],
        device_id={axis: peer}, device_id_type=MESH,
    )


def share_start(axis, value, slots, send_sem, recv_sem):
    slots[lax.axis_index(axis)] = value
    for offset in range(1, lax.axis_size(axis)):
        share_copy(axis, slots, send_sem, recv_sem, offset, False).start()


def share_finish(axis, slots, send_sem, recv_sem):
    for offset in range(1, lax.axis_size(axis)):
        share_copy(axis, slots, send_sem, recv_sem, offset, True).wait_recv()
    for offset in range(1, lax.axis_size(axis)):
        share_copy(axis, slots, send_sem, recv_sem, offset, False).wait_send()


def share(axis, value, slots, send_sem, recv_sem):
    share_start(axis, value, slots, send_sem, recv_sem)
    share_finish(axis, slots, send_sem, recv_sem)


def added(slots):
    total = slots[0]
    for slot in range(1, slots.shape[0]):
        total = total + slots[slot]
    return total


def backward_part(vectors, matrix_ref):
    systems = vectors.shape[0]
    squares = jnp.sum(vectors * vectors, axis=1, keepdims=True)
    product = jnp.dot(split_rows(vectors), matrix_ref[...], preferred_element_type=jnp.float32)
    return jnp.concatenate(
        [join_rows(product, systems), jnp.broadcast_to(squares, (systems, matrix_ref.shape[1]))], axis=0
    )


def split_rows(vectors):
    top = vectors.astype(jnp.bfloat16).astype(jnp.float32)
    rest = vectors - top
    middle = rest.astype(jnp.bfloat16).astype(jnp.float32)
    low = rest - middle
    return jnp.concatenate([top, middle, low, jnp.zeros_like(low)], axis=0).astype(jnp.bfloat16)


def join_rows(stacked, systems):
    return stacked[:systems] + stacked[systems:2 * systems] + stacked[2 * systems:3 * systems]


def lsqr_kernel(
    matrix_ref, inverse_ref, right_ref, first_ref, norm_ref, solution_ref, residual_ref,
    row_slots, col_slots, image_slots, norm_slots,
    row_send, row_recv, col_send, col_recv, image_send, image_recv, norm_send, norm_recv,
):
    systems = right_ref.shape[0]
    col_count = matrix_ref.shape[1]
    own = pl.ds(pl.multiple_of(lax.axis_index("cols") * col_count, col_count), col_count)
    greet(("rows", "cols"))

    def forward(own_part, turn):
        product = lax.dot_general(
            split_rows(own_part), matrix_ref[...], (((1,), (1,)), ((), ())),
            preferred_element_type=jnp.float32,
        )
        share("cols", join_rows(product, systems), image_slots.at[turn], image_send.at[turn], image_recv.at[turn])
        return added(image_slots.at[turn])

    def backward(vectors, turn):
        share("rows", backward_part(vectors, matrix_ref), row_slots.at[turn], row_send.at[turn], row_recv.at[turn])
        total = added(row_slots.at[turn])
        norm = jnp.sqrt(total[systems:, 0:1])
        share("cols", total[:systems] / norm, col_slots.at[turn], col_send.at[turn], col_recv.at[turn])
        whole = jnp.concatenate([col_slots[turn, slot] for slot in range(col_slots.shape[1])], axis=1)
        return norm, whole

    def solve_right(vectors):
        return lax.dot_general(
            vectors, inverse_ref[...], (((1,), (1,)), ((), ())),
            precision=highest, preferred_element_type=jnp.float32,
        )

    def solve_left(vectors):
        return jnp.dot(vectors, inverse_ref[:, own], precision=highest, preferred_element_type=jnp.float32)

    def norm_of(vectors):
        return jnp.sqrt(jnp.sum(vectors * vectors, axis=1, keepdims=True))

    right_sides = right_ref[...]
    beta_norm = norm_ref[:, 0:1]
    whole_vector = jnp.concatenate([first_ref[slot] for slot in range(first_ref.shape[0])], axis=1)
    left_unit = right_sides / beta_norm
    back_rest = solve_right(whole_vector)
    alpha_norm = norm_of(back_rest)
    right_unit = back_rest / alpha_norm
    moved = solve_left(right_unit)
    image = forward(moved, 0)
    search, search_image = moved, image
    coeffs = jnp.zeros_like(moved)
    coeffs_image = jnp.zeros_like(image)
    phibar = beta_norm
    rhobar = alpha_norm
    for iteration in range(ROUNDS):
        last = iteration == ROUNDS - 1
        forward_rest = image - alpha_norm * left_unit
        if last:
            squares = jnp.sum(forward_rest * forward_rest, axis=1, keepdims=True)
            share("rows", jnp.broadcast_to(squares, norm_slots.shape[1:]), norm_slots, norm_send, norm_recv)
            beta_norm = jnp.sqrt(added(norm_slots)[:, 0:1])
        else:
            beta_norm, whole_vector = backward(forward_rest, iteration)
        rho_total = jnp.sqrt(rhobar * rhobar + beta_norm * beta_norm)
        cosine = rhobar / rho_total
        sine_part = beta_norm / rho_total
        ratio = cosine * phibar / rho_total
        coeffs = coeffs + ratio * search
        coeffs_image = coeffs_image + ratio * search_image
        if last:
            break
        left_unit = forward_rest / beta_norm
        back_rest = solve_right(whole_vector) - beta_norm * right_unit
        alpha_norm = norm_of(back_rest)
        right_unit = back_rest / alpha_norm
        moved = solve_left(right_unit)
        image = forward(moved, iteration + 1)
        shrink = sine_part * alpha_norm / rho_total
        rhobar = -cosine * alpha_norm
        phibar = sine_part * phibar
        search = moved - shrink * search
        search_image = image - shrink * search_image
    solution_ref[...] = coeffs
    residual_ref[...] = right_sides - coeffs_image


def lsqr(matrix, inverse, right_sides, first, norm):
    row_count, col_count = matrix.shape
    systems = right_sides.shape[0]
    row_size, col_size = lax.axis_size("rows"), lax.axis_size("cols")
    vmem = pl.BlockSpec(memory_space=pltpu.VMEM)
    dma = pltpu.SemaphoreType.DMA
    return pl.pallas_call(
        lsqr_kernel,
        out_shape=(
            jax.ShapeDtypeStruct((systems, col_count), jnp.float32),
            jax.ShapeDtypeStruct((systems, row_count), jnp.float32),
        ),
        in_specs=[vmem] * 5,
        out_specs=(vmem, vmem),
        scratch_shapes=[
            pltpu.VMEM((ROUNDS - 1, row_size, 2 * systems, col_count), jnp.float32),
            pltpu.VMEM((ROUNDS - 1, col_size, systems, col_count), jnp.float32),
            pltpu.VMEM((ROUNDS, col_size, systems, row_count), jnp.float32),
            pltpu.VMEM((row_size, systems, 128), jnp.float32),
            dma((ROUNDS - 1, row_size)), dma((ROUNDS - 1, row_size)),
            dma((ROUNDS - 1, col_size)), dma((ROUNDS - 1, col_size)),
            dma((ROUNDS, col_size)), dma((ROUNDS, col_size)),
            dma((row_size,)), dma((row_size,)),
        ],
        compiler_params=pltpu.CompilerParams(
            collective_id=0, has_side_effects=True, vmem_limit_bytes=40 * 1024 * 1024
        ),
    )(matrix, inverse, right_sides, first, norm)


def picked_mixer(sampled, row_count):
    count = sampled.shape[0]
    lanes = min(128, row_count)
    common = sampled & lax.broadcasted_iota(jnp.int32, (count, lanes), 1)
    for shift in (4, 2, 1):
        common = common ^ lax.shift_right_logical(common, shift)
    mixer = jnp.where((common & 1) == 0, 1.0, -1.0).astype(jnp.float32)
    width = lanes
    while width < row_count:
        sign = jnp.where((sampled & width) == 0, 1.0, -1.0).astype(jnp.float32)
        mixer = jnp.concatenate([mixer, mixer * sign], axis=1)
        width = 2 * width
    return mixer.astype(jnp.bfloat16)


def col_bits(size):
    return [1 << place for place in range(size.bit_length() - 2, -1, -1)]


def gram_kernel(
    signed_ref, sampled_ref, matrix_ref, right_ref, gram_ref, first_ref, norm_ref,
    sketch_out, sketch_near, sketch_sum, sketch_far, pieces, partial,
    gram_out, gram_near, gram_sum, gram_far, row_slots,
    near_send, near_recv, far_send, far_recv, piece_send, piece_recv,
    block_send, block_recv, block_far_send, row_send, row_recv, col_send, col_recv,
):
    row_size, col_size = lax.axis_size("rows"), lax.axis_size("cols")
    row, col = lax.axis_index("rows"), lax.axis_index("cols")
    inner_size = 2 if row_size % 2 == 0 else 1
    outer_size = row_size // inner_size
    inner, outer = lax.rem(row, inner_size), row // inner_size
    row_count, col_count = signed_ref.shape
    sketch_rows = sampled_ref.shape[0]
    systems = right_ref.shape[0]
    bits = col_bits(col_size)
    started = []

    def flip(place, bit):
        return place + bit - 2 * bit * lax.rem(place // bit, 2)

    def start(source, target, send_sem, recv_sem, device):
        copy = pltpu.make_async_remote_copy(
            src_ref=source, dst_ref=target, send_sem=send_sem, recv_sem=recv_sem,
            device_id=device, device_id_type=MESH,
        )
        copy.start()
        started.append(copy)

    def arrived(target, recv_sem, device):
        pltpu.make_async_remote_copy(
            src_ref=target, dst_ref=target, send_sem=recv_sem, recv_sem=recv_sem,
            device_id=device, device_id_type=MESH,
        ).wait_recv()

    near_peer = {"rows": outer * inner_size + (inner_size - 1 - inner)}
    outer_order = [lax.rem(outer + step, outer_size) for step in range(1, outer_size)] + [outer]

    def reduce_scatter(turn, chunk, out, near, summed, far):
        if inner_size == 2:
            for other in outer_order:
                out[other] = chunk(other * inner_size + 1 - inner)
                start(out.at[other], near.at[other], near_send.at[turn, other], near_recv.at[turn, other], near_peer)
        total = None
        for step, other in enumerate(outer_order):
            total = chunk(other * inner_size + inner)
            if inner_size == 2:
                arrived(near.at[other], near_recv.at[turn, other], near_peer)
                total = total + near[other]
            if step < outer_size - 1:
                summed[other] = total
                start(
                    summed.at[other], far.at[outer], far_send.at[turn, other], far_recv.at[turn, outer],
                    {"rows": other * inner_size + inner},
                )
        for offset in range(1, outer_size):
            source = lax.rem(outer + outer_size - offset, outer_size)
            arrived(far.at[source], far_recv.at[turn, source], {"rows": source * inner_size + inner})
            total = total + far[source]
        return total

    greet(("rows", "cols"))

    share_start("rows", backward_part(right_ref[...], matrix_ref), row_slots, row_send, row_recv)

    piece_rows = sketch_rows // row_size

    def sketch_chunk(target):
        sampled = sampled_ref[pl.ds(pl.multiple_of(target * piece_rows, piece_rows), piece_rows), :]
        return jnp.dot(
            picked_mixer(sampled, row_count), signed_ref[...], preferred_element_type=jnp.float32
        ) * (1.0 / math.sqrt(sketch_rows))

    own_piece = reduce_scatter(0, sketch_chunk, sketch_out, sketch_near, sketch_sum, sketch_far)
    pieces[col] = own_piece
    for place, bit in enumerate(bits):
        start(pieces.at[col], pieces.at[col], piece_send.at[place, col], piece_recv.at[col], {"cols": flip(col, bit)})

    share_finish("rows", row_slots, row_send, row_recv)
    first_total = added(row_slots)
    first_norm = jnp.sqrt(first_total[systems:])
    norm_ref[...] = first_norm[:, :norm_ref.shape[1]]
    share_start("cols", first_total[:systems] / first_norm, first_ref, col_send, col_recv)

    masks = sorted(range(1, col_size), key=lambda mask: (-(mask & -mask), mask))

    def other_col(mask):
        place = col
        for bit in bits:
            if mask & bit:
                place = flip(place, bit)
        return place

    def multiply(block):
        partial[pl.ds(pl.multiple_of(block * col_count, col_count), col_count), :] = lax.dot_general(
            pieces[block], pieces[col], (((0,), (0,)), ((), ())),
            precision=highest, preferred_element_type=jnp.float32,
        )

    multiply(col)
    for mask in masks:
        block = other_col(mask)
        arrived(pieces.at[block], piece_recv.at[block], {"cols": flip(col, mask & -mask)})
        for place, bit in enumerate(bits):
            if bit < (mask & -mask):
                start(
                    pieces.at[block], pieces.at[block], piece_send.at[place, block], piece_recv.at[block],
                    {"cols": flip(col, bit)},
                )
        multiply(block)

    block_rows = gram_ref.shape[1] // row_size

    def rows_of(target):
        return pl.ds(pl.multiple_of(target * block_rows, block_rows), block_rows)

    total = reduce_scatter(
        1, lambda target: partial[rows_of(target), :], gram_out, gram_near, gram_sum, gram_far
    )

    def block_ref(block_row, block_col):
        return gram_ref.at[block_col, rows_of(block_row), :]

    def pass_on(block_row, block_col, below):
        for place, bit in enumerate(bits):
            if bit < below:
                start(
                    block_ref(block_row, block_col), block_ref(block_row, block_col),
                    block_send.at[place, block_row, block_col], block_recv.at[block_row, block_col],
                    {"cols": flip(col, bit)},
                )

    def pass_near(block_row):
        if inner_size == 2:
            start(
                block_ref(block_row, col), block_ref(block_row, col),
                block_send.at[len(bits), block_row, col], block_recv.at[block_row, col], near_peer,
            )

    gram_ref[col, rows_of(row), :] = total
    for offset in range(1, outer_size):
        other = lax.rem(outer + offset, outer_size)
        start(
            block_ref(row, col), block_ref(row, col), block_far_send.at[offset], block_recv.at[row, col],
            {"rows": other * inner_size + inner},
        )
    pass_near(row)
    pass_on(row, col, col_size)
    for offset in range(1, outer_size):
        source = lax.rem(outer + outer_size - offset, outer_size) * inner_size + inner
        arrived(block_ref(source, col), block_recv.at[source, col], {"rows": source})
        pass_near(source)
        pass_on(source, col, col_size)
    by_distance = [lax.rem(outer + outer_size - offset, outer_size) for offset in range(outer_size)]
    if inner_size == 2:
        for other in by_distance:
            source = other * inner_size + 1 - inner
            arrived(block_ref(source, col), block_recv.at[source, col], near_peer)
            pass_on(source, col, col_size)
    for mask in masks:
        block = other_col(mask)
        for layer in range(inner_size):
            for other in by_distance:
                source = other * inner_size + (inner if layer == 0 else 1 - inner)
                arrived(block_ref(source, block), block_recv.at[source, block], {"cols": flip(col, mask & -mask)})
                pass_on(source, block, mask & -mask)
    share_finish("cols", first_ref, col_send, col_recv)
    for copy in started:
        copy.wait_send()


def sketched_gram(signed, sampled, matrix, right_sides):
    row_count, col_count = matrix.shape
    systems = right_sides.shape[0]
    sketch_rows = sampled.shape[0]
    row_size, col_size = lax.axis_size("rows"), lax.axis_size("cols")
    inner_size = 2 if row_size % 2 == 0 else 1
    outer_size = row_size // inner_size
    order = col_count * col_size
    bit_total = max(len(col_bits(col_size)), 1)
    vmem = pl.BlockSpec(memory_space=pltpu.VMEM)
    dma = pltpu.SemaphoreType.DMA
    float_vmem = lambda *shape: pltpu.VMEM(shape, jnp.float32)
    return pl.pallas_call(
        gram_kernel,
        out_shape=(
            jax.ShapeDtypeStruct((col_size, order, col_count), jnp.float32),
            jax.ShapeDtypeStruct((col_size, systems, col_count), jnp.float32),
            jax.ShapeDtypeStruct((systems, 128), jnp.float32),
        ),
        in_specs=[vmem] * 4,
        out_specs=(vmem, vmem, vmem),
        scratch_shapes=[float_vmem(outer_size, sketch_rows // row_size, col_count)] * 4
        + [float_vmem(col_size, sketch_rows // row_size, col_count), float_vmem(order, col_count)]
        + [float_vmem(outer_size, order // row_size, col_count)] * 4
        + [
            float_vmem(row_size, 2 * systems, col_count),
            dma((2, outer_size)), dma((2, outer_size)), dma((2, outer_size)), dma((2, outer_size)),
            dma((bit_total, col_size)), dma((col_size,)),
            dma((bit_total + 1, row_size, col_size)), dma((row_size, col_size)), dma((outer_size,)),
            dma((row_size,)), dma((row_size,)), dma((col_size,)), dma((col_size,)),
        ],
        compiler_params=pltpu.CompilerParams(
            collective_id=1, has_side_effects=True, vmem_limit_bytes=48 * 1024 * 1024
        ),
    )(signed, sampled, matrix, right_sides)


def local(matrix, row_signs, sampled_rows, right_sides):
    signed = matrix * (1 - 2 * row_signs).astype(jnp.bfloat16)[:, None]
    sampled = sampled_rows.reshape(-1, 1)
    gram_matrix, first, norm = sketched_gram(signed, sampled, matrix, right_sides)
    inverse = inverse_factor(gram_matrix)
    return lsqr(matrix, inverse, right_sides, first, norm)


def solution(mesh):
    in_specs = (P("rows", "cols"), P("rows"), P("rows", None), P(None, "rows"))
    out_specs = (P(None, "cols"), P(None, "rows"))
    return jax.shard_map(local, mesh=mesh, in_specs=in_specs, out_specs=out_specs, check_vma=False)
```

```python
import functools
import math

import jax
import jax.numpy as jnp
from jax import lax
from jax.experimental import pallas as pl
from jax.experimental.pallas import tpu as pltpu
from jax.sharding import PartitionSpec as P

ROUNDS = 2
BLOCK = 128
STRIP = 8

highest = lax.Precision.HIGHEST


def block_inverse(square):
    size = square.shape[0]
    row_ids = lax.broadcasted_iota(jnp.int32, (size, size), 0)
    col_ids = lax.broadcasted_iota(jnp.int32, (size, size), 1)
    rest = square
    unit = jnp.where(row_ids == col_ids, 1.0, 0.0).astype(jnp.float32)
    finished = []
    for strip in range(size // STRIP):
        start = strip * STRIP
        height = size - start
        here = lax.broadcasted_iota(jnp.int32, (height, size), 0)
        columns = [
            jnp.broadcast_to(rest[:, start + k:start + k + 1], (height, size)) for k in range(STRIP)
        ]
        scale = jnp.ones((STRIP, size), jnp.float32)
        for k in range(STRIP):
            pivot = columns[k][k:k + 1, :]
            factors = jnp.where(here > k, columns[k] * (1.0 / pivot), 0.0)
            for later in range(k + 1, STRIP):
                columns[later] = columns[later] - factors * columns[later][k:k + 1, :]
            rest = rest - factors * rest[k:k + 1, :]
            unit = unit - factors * unit[k:k + 1, :]
            scale = jnp.where(here[:STRIP] == k, lax.rsqrt(pivot), scale)
        finished.append(unit[:STRIP] * scale)
        rest = rest[STRIP:]
        unit = unit[STRIP:]
    return jnp.concatenate(finished, axis=0)


def inverse_factor_kernel(gram_ref, out_ref, strip_ref):
    order = out_ref.shape[0]
    blocks = order // BLOCK
    col_size, _, width = gram_ref.shape
    half = width // 2
    for col in range(col_size):
        for other in range(col_size):
            low, high = min(col, other), max(col, other)
            start = low * width + (half if col > other else 0)
            if col == other:
                out_ref[start:start + width, high * width:(high + 1) * width] = gram_ref[col, :width, :]
                continue
            place = width + half * ((col ^ other) - 1)
            out_ref[start:start + half, high * width:(high + 1) * width] = gram_ref[col, place:place + half, :]
            if col > other:
                out_ref[col * width:(col + 1) * width, other * width:(other + 1) * width] = jnp.zeros(
                    (width, width), jnp.float32
                )

    def step(block, carry):
        start = pl.multiple_of(block * BLOCK, BLOCK)
        own = pl.ds(start, BLOCK)
        inverse = block_inverse(out_ref[own, own])
        strip_ref[...] = jnp.dot(
            inverse, out_ref[own, :], precision=highest, preferred_element_type=jnp.float32
        )
        strip_ref[:, own] = inverse

        def update(row_block, inner):
            rows = pl.ds(pl.multiple_of(row_block * BLOCK, BLOCK), BLOCK)
            out_ref[rows, own] = jnp.zeros((BLOCK, BLOCK), jnp.float32)
            out_ref[rows, :] = out_ref[rows, :] - lax.dot_general(
                strip_ref[:, rows], strip_ref[...], (((0,), (0,)), ((), ())),
                precision=highest, preferred_element_type=jnp.float32,
            )
            return inner

        lax.fori_loop(block + 1, blocks, update, 0)
        col_ids = lax.broadcasted_iota(jnp.int32, (BLOCK, order), 1)
        out_ref[own, :] = jnp.where(col_ids < start + BLOCK, strip_ref[...], 0.0)
        return carry

    lax.fori_loop(0, blocks, step, 0)


def inverse_factor(gram_matrix):
    order = gram_matrix.shape[0] * gram_matrix.shape[2]
    return pl.pallas_call(
        inverse_factor_kernel,
        out_shape=jax.ShapeDtypeStruct((order, order), jnp.float32),
        in_specs=[pl.BlockSpec(memory_space=pltpu.VMEM)],
        out_specs=pl.BlockSpec(memory_space=pltpu.VMEM),
        scratch_shapes=[pltpu.VMEM((BLOCK, order), jnp.float32)],
        compiler_params=pltpu.CompilerParams(vmem_limit_bytes=32 * 1024 * 1024),
    )(gram_matrix)


MESH = pl.DeviceIdType.MESH


def greet(axes):
    barrier = pltpu.get_barrier_semaphore()
    count = 0
    for axis in axes:
        size = lax.axis_size(axis)
        me = lax.axis_index(axis)
        for offset in range(1, size):
            pl.semaphore_signal(
                barrier, inc=1, device_id={axis: lax.rem(me + offset, size)}, device_id_type=MESH
            )
        count += size - 1
    pl.semaphore_wait(barrier, count)


def share_copy(axis, slots, send_sem, recv_sem, offset, incoming):
    size = lax.axis_size(axis)
    me = lax.axis_index(axis)
    peer = lax.rem(me + (size - offset if incoming else offset), size)
    slot = peer if incoming else me
    return pltpu.make_async_remote_copy(
        src_ref=slots.at[slot], dst_ref=slots.at[slot],
        send_sem=send_sem.at[offset - 1], recv_sem=recv_sem.at[slot],
        device_id={axis: peer}, device_id_type=MESH,
    )


def share_start(axis, value, slots, send_sem, recv_sem):
    slots[lax.axis_index(axis)] = value
    for offset in range(1, lax.axis_size(axis)):
        share_copy(axis, slots, send_sem, recv_sem, offset, False).start()


def share_finish(axis, slots, send_sem, recv_sem):
    for offset in range(1, lax.axis_size(axis)):
        share_copy(axis, slots, send_sem, recv_sem, offset, True).wait_recv()
    for offset in range(1, lax.axis_size(axis)):
        share_copy(axis, slots, send_sem, recv_sem, offset, False).wait_send()


def share(axis, value, slots, send_sem, recv_sem):
    share_start(axis, value, slots, send_sem, recv_sem)
    share_finish(axis, slots, send_sem, recv_sem)


def added(slots):
    total = slots[0]
    for slot in range(1, slots.shape[0]):
        total = total + slots[slot]
    return total


def backward_part(vectors, matrix_ref):
    systems = vectors.shape[0]
    squares = jnp.sum(vectors * vectors, axis=1, keepdims=True)
    product = jnp.dot(split_rows(vectors), matrix_ref[...], preferred_element_type=jnp.float32)
    return jnp.concatenate(
        [join_rows(product, systems), jnp.broadcast_to(squares, (systems, matrix_ref.shape[1]))], axis=0
    )


def split_rows(vectors):
    top = vectors.astype(jnp.bfloat16).astype(jnp.float32)
    rest = vectors - top
    middle = rest.astype(jnp.bfloat16).astype(jnp.float32)
    low = rest - middle
    return jnp.concatenate([top, middle, low, jnp.zeros_like(low)], axis=0).astype(jnp.bfloat16)


def join_rows(stacked, systems):
    return stacked[:systems] + stacked[systems:2 * systems] + stacked[2 * systems:3 * systems]


def lsqr_kernel(
    matrix_ref, inverse_ref, right_ref, first_ref, norm_ref, solution_ref, residual_ref,
    row_slots, col_slots, image_slots, norm_slots,
    row_send, row_recv, col_send, col_recv, image_send, image_recv, norm_send, norm_recv,
):
    systems = right_ref.shape[0]
    col_count = matrix_ref.shape[1]
    own = pl.ds(pl.multiple_of(lax.axis_index("cols") * col_count, col_count), col_count)
    greet(("rows", "cols"))

    def forward(own_part, turn):
        product = lax.dot_general(
            split_rows(own_part), matrix_ref[...], (((1,), (1,)), ((), ())),
            preferred_element_type=jnp.float32,
        )
        share("cols", join_rows(product, systems), image_slots.at[turn], image_send.at[turn], image_recv.at[turn])
        return added(image_slots.at[turn])

    def backward(vectors, turn):
        share("rows", backward_part(vectors, matrix_ref), row_slots.at[turn], row_send.at[turn], row_recv.at[turn])
        total = added(row_slots.at[turn])
        norm = jnp.sqrt(total[systems:, 0:1])
        share("cols", total[:systems] / norm, col_slots.at[turn], col_send.at[turn], col_recv.at[turn])
        whole = jnp.concatenate([col_slots[turn, slot] for slot in range(col_slots.shape[1])], axis=1)
        return norm, whole

    def solve_right(vectors):
        return lax.dot_general(
            vectors, inverse_ref[...], (((1,), (1,)), ((), ())),
            precision=highest, preferred_element_type=jnp.float32,
        )

    def solve_left(vectors):
        return jnp.dot(vectors, inverse_ref[:, own], precision=highest, preferred_element_type=jnp.float32)

    def norm_of(vectors):
        return jnp.sqrt(jnp.sum(vectors * vectors, axis=1, keepdims=True))

    right_sides = right_ref[...]
    beta_norm = norm_ref[:, 0:1]
    whole_vector = jnp.concatenate([first_ref[slot] for slot in range(first_ref.shape[0])], axis=1)
    left_unit = right_sides / beta_norm
    back_rest = solve_right(whole_vector)
    alpha_norm = norm_of(back_rest)
    right_unit = back_rest / alpha_norm
    moved = solve_left(right_unit)
    image = forward(moved, 0)
    search, search_image = moved, image
    coeffs = jnp.zeros_like(moved)
    coeffs_image = jnp.zeros_like(image)
    phibar = beta_norm
    rhobar = alpha_norm
    for iteration in range(ROUNDS):
        last = iteration == ROUNDS - 1
        forward_rest = image - alpha_norm * left_unit
        if last:
            squares = jnp.sum(forward_rest * forward_rest, axis=1, keepdims=True)
            share("rows", jnp.broadcast_to(squares, norm_slots.shape[1:]), norm_slots, norm_send, norm_recv)
            beta_norm = jnp.sqrt(added(norm_slots)[:, 0:1])
        else:
            beta_norm, whole_vector = backward(forward_rest, iteration)
        rho_total = jnp.sqrt(rhobar * rhobar + beta_norm * beta_norm)
        cosine = rhobar / rho_total
        sine_part = beta_norm / rho_total
        ratio = cosine * phibar / rho_total
        coeffs = coeffs + ratio * search
        coeffs_image = coeffs_image + ratio * search_image
        if last:
            break
        left_unit = forward_rest / beta_norm
        back_rest = solve_right(whole_vector) - beta_norm * right_unit
        alpha_norm = norm_of(back_rest)
        right_unit = back_rest / alpha_norm
        moved = solve_left(right_unit)
        image = forward(moved, iteration + 1)
        shrink = sine_part * alpha_norm / rho_total
        rhobar = -cosine * alpha_norm
        phibar = sine_part * phibar
        search = moved - shrink * search
        search_image = image - shrink * search_image
    solution_ref[...] = coeffs
    residual_ref[...] = right_sides - coeffs_image


def lsqr(matrix, inverse, right_sides, first, norm):
    row_count, col_count = matrix.shape
    systems = right_sides.shape[0]
    row_size, col_size = lax.axis_size("rows"), lax.axis_size("cols")
    vmem = pl.BlockSpec(memory_space=pltpu.VMEM)
    dma = pltpu.SemaphoreType.DMA
    return pl.pallas_call(
        lsqr_kernel,
        out_shape=(
            jax.ShapeDtypeStruct((systems, col_count), jnp.float32),
            jax.ShapeDtypeStruct((systems, row_count), jnp.float32),
        ),
        in_specs=[vmem] * 5,
        out_specs=(vmem, vmem),
        scratch_shapes=[
            pltpu.VMEM((ROUNDS - 1, row_size, 2 * systems, col_count), jnp.float32),
            pltpu.VMEM((ROUNDS - 1, col_size, systems, col_count), jnp.float32),
            pltpu.VMEM((ROUNDS, col_size, systems, row_count), jnp.float32),
            pltpu.VMEM((row_size, systems, 128), jnp.float32),
            dma((ROUNDS - 1, row_size)), dma((ROUNDS - 1, row_size)),
            dma((ROUNDS - 1, col_size)), dma((ROUNDS - 1, col_size)),
            dma((ROUNDS, col_size)), dma((ROUNDS, col_size)),
            dma((row_size,)), dma((row_size,)),
        ],
        compiler_params=pltpu.CompilerParams(
            collective_id=0, has_side_effects=True, vmem_limit_bytes=40 * 1024 * 1024
        ),
    )(matrix, inverse, right_sides, first, norm)


def picked_mixer(sampled, signs):
    row_count = signs.shape[1]
    count = sampled.shape[0]
    lanes = min(128, row_count)
    common = sampled & lax.broadcasted_iota(jnp.int32, (count, lanes), 1)
    for shift in (4, 2, 1):
        common = common ^ lax.shift_right_logical(common, shift)
    mixer = jnp.where((common & 1) == 0, 1.0, -1.0).astype(jnp.float32)
    width = lanes
    while width < row_count:
        sign = jnp.where((sampled & width) == 0, 1.0, -1.0).astype(jnp.float32)
        mixer = jnp.concatenate([mixer, mixer * sign], axis=1)
        width = 2 * width
    return (mixer * signs).astype(jnp.bfloat16)


def col_bits(size):
    return [1 << place for place in range(size.bit_length() - 2, -1, -1)]


def gram_kernel(
    signs_ref, sampled_ref, matrix_ref, right_ref, gram_ref, first_ref, norm_ref,
    sketch_out, sketch_near, sketch_sum, sketch_far, pieces, partial,
    gram_out, gram_near, gram_sum, gram_far, row_slots,
    near_send, near_recv, far_send, far_recv, piece_send, piece_recv,
    block_send, block_recv, block_far_send, row_send, row_recv, col_send, col_recv,
):
    row_size, col_size = lax.axis_size("rows"), lax.axis_size("cols")
    row, col = lax.axis_index("rows"), lax.axis_index("cols")
    inner_size = 2 if row_size % 2 == 0 else 1
    outer_size = row_size // inner_size
    inner, outer = lax.rem(row, inner_size), row // inner_size
    col_count = matrix_ref.shape[1]
    sketch_rows = sampled_ref.shape[0]
    systems = right_ref.shape[0]
    bits = col_bits(col_size)
    started = []

    def flip(place, bit):
        return place + bit - 2 * bit * lax.rem(place // bit, 2)

    def start(source, target, send_sem, recv_sem, device):
        copy = pltpu.make_async_remote_copy(
            src_ref=source, dst_ref=target, send_sem=send_sem, recv_sem=recv_sem,
            device_id=device, device_id_type=MESH,
        )
        copy.start()
        started.append(copy)

    def arrived(target, recv_sem, device):
        pltpu.make_async_remote_copy(
            src_ref=target, dst_ref=target, send_sem=recv_sem, recv_sem=recv_sem,
            device_id=device, device_id_type=MESH,
        ).wait_recv()

    near_peer = {"rows": outer * inner_size + (inner_size - 1 - inner)}
    outer_order = [lax.rem(outer + step, outer_size) for step in range(1, outer_size)] + [outer]

    def reduce_scatter(turn, chunk, out, near, summed, far):
        if inner_size == 2:
            for other in outer_order:
                out[other] = chunk(other * inner_size + 1 - inner)
                start(out.at[other], near.at[other], near_send.at[turn, other], near_recv.at[turn, other], near_peer)
        total = None
        for step, other in enumerate(outer_order):
            total = chunk(other * inner_size + inner)
            if inner_size == 2:
                arrived(near.at[other], near_recv.at[turn, other], near_peer)
                total = total + near[other]
            if step < outer_size - 1:
                summed[other] = total
                start(
                    summed.at[other], far.at[outer], far_send.at[turn, other], far_recv.at[turn, outer],
                    {"rows": other * inner_size + inner},
                )
        for offset in range(1, outer_size):
            source = lax.rem(outer + outer_size - offset, outer_size)
            arrived(far.at[source], far_recv.at[turn, source], {"rows": source * inner_size + inner})
            total = total + far[source]
        return total

    greet(("rows", "cols"))

    share_start("rows", backward_part(right_ref[...], matrix_ref), row_slots, row_send, row_recv)

    piece_rows = sketch_rows // row_size

    signs = (1 - 2 * signs_ref[...]).astype(jnp.float32)

    def sketch_chunk(target):
        sampled = sampled_ref[pl.ds(pl.multiple_of(target * piece_rows, piece_rows), piece_rows), :]
        return jnp.dot(
            picked_mixer(sampled, signs), matrix_ref[...], preferred_element_type=jnp.float32
        ) * (1.0 / math.sqrt(sketch_rows))

    own_piece = reduce_scatter(0, sketch_chunk, sketch_out, sketch_near, sketch_sum, sketch_far)
    pieces[col] = own_piece
    for place, bit in enumerate(bits):
        start(pieces.at[col], pieces.at[col], piece_send.at[place, col], piece_recv.at[col], {"cols": flip(col, bit)})

    share_finish("rows", row_slots, row_send, row_recv)
    first_total = added(row_slots)
    first_norm = jnp.sqrt(first_total[systems:])
    norm_ref[...] = first_norm[:, :norm_ref.shape[1]]
    share_start("cols", first_total[:systems] / first_norm, first_ref, col_send, col_recv)

    masks = sorted(range(1, col_size), key=lambda mask: (-(mask & -mask), mask))

    def other_col(mask):
        place = col
        for bit in bits:
            if mask & bit:
                place = flip(place, bit)
        return place

    half = col_count // 2

    def product(left, right):
        return lax.dot_general(
            left, right, (((0,), (0,)), ((), ())), precision=highest, preferred_element_type=jnp.float32
        )

    def multiply(mask, block):
        top = 1 << (mask.bit_length() - 1)
        upper = lax.rem(col // top, 2)
        low = col - upper * (col - block)
        high = col + block - low
        place = col_count + half * (mask - 1)
        partial[place:place + half, :] = product(
            pieces[low, :, pl.ds(pl.multiple_of(upper * half, half), half)], pieces[high]
        )

    partial[:col_count, :] = product(own_piece, own_piece)
    used = col_count + half * (col_size - 1)
    if used < partial.shape[0]:
        partial[used:, :] = jnp.zeros((partial.shape[0] - used, col_count), jnp.float32)
    for mask in masks:
        block = other_col(mask)
        arrived(pieces.at[block], piece_recv.at[block], {"cols": flip(col, mask & -mask)})
        for place, bit in enumerate(bits):
            if bit < (mask & -mask):
                start(
                    pieces.at[block], pieces.at[block], piece_send.at[place, block], piece_recv.at[block],
                    {"cols": flip(col, bit)},
                )
        multiply(mask, block)

    block_rows = gram_ref.shape[1] // row_size

    def rows_of(target):
        return pl.ds(pl.multiple_of(target * block_rows, block_rows), block_rows)

    total = reduce_scatter(
        1, lambda target: partial[rows_of(target), :], gram_out, gram_near, gram_sum, gram_far
    )

    def block_ref(block_row, block_col):
        return gram_ref.at[block_col, rows_of(block_row), :]

    def pass_on(block_row, block_col, below):
        for place, bit in enumerate(bits):
            if bit < below:
                start(
                    block_ref(block_row, block_col), block_ref(block_row, block_col),
                    block_send.at[place, block_row, block_col], block_recv.at[block_row, block_col],
                    {"cols": flip(col, bit)},
                )

    def pass_near(block_row):
        if inner_size == 2:
            start(
                block_ref(block_row, col), block_ref(block_row, col),
                block_send.at[len(bits), block_row, col], block_recv.at[block_row, col], near_peer,
            )

    gram_ref[col, rows_of(row), :] = total
    for offset in range(1, outer_size):
        other = lax.rem(outer + offset, outer_size)
        start(
            block_ref(row, col), block_ref(row, col), block_far_send.at[offset], block_recv.at[row, col],
            {"rows": other * inner_size + inner},
        )
    pass_near(row)
    pass_on(row, col, col_size)
    for offset in range(1, outer_size):
        source = lax.rem(outer + outer_size - offset, outer_size) * inner_size + inner
        arrived(block_ref(source, col), block_recv.at[source, col], {"rows": source})
        pass_near(source)
        pass_on(source, col, col_size)
    by_distance = [lax.rem(outer + outer_size - offset, outer_size) for offset in range(outer_size)]
    if inner_size == 2:
        for other in by_distance:
            source = other * inner_size + 1 - inner
            arrived(block_ref(source, col), block_recv.at[source, col], near_peer)
            pass_on(source, col, col_size)
    for mask in masks:
        block = other_col(mask)
        for layer in range(inner_size):
            for other in by_distance:
                source = other * inner_size + (inner if layer == 0 else 1 - inner)
                arrived(block_ref(source, block), block_recv.at[source, block], {"cols": flip(col, mask & -mask)})
                pass_on(source, block, mask & -mask)
    share_finish("cols", first_ref, col_send, col_recv)
    for copy in started:
        copy.wait_send()


def sketched_gram(row_signs, sampled, matrix, right_sides):
    row_count, col_count = matrix.shape
    systems = right_sides.shape[0]
    sketch_rows = sampled.shape[0]
    row_size, col_size = lax.axis_size("rows"), lax.axis_size("cols")
    inner_size = 2 if row_size % 2 == 0 else 1
    outer_size = row_size // inner_size
    used = col_count + col_count // 2 * (col_size - 1)
    stack = row_size * STRIP * pl.cdiv(used, row_size * STRIP)
    bit_total = max(len(col_bits(col_size)), 1)
    vmem = pl.BlockSpec(memory_space=pltpu.VMEM)
    dma = pltpu.SemaphoreType.DMA
    float_vmem = lambda *shape: pltpu.VMEM(shape, jnp.float32)
    return pl.pallas_call(
        gram_kernel,
        out_shape=(
            jax.ShapeDtypeStruct((col_size, stack, col_count), jnp.float32),
            jax.ShapeDtypeStruct((col_size, systems, col_count), jnp.float32),
            jax.ShapeDtypeStruct((systems, 128), jnp.float32),
        ),
        in_specs=[vmem] * 4,
        out_specs=(vmem, vmem, vmem),
        scratch_shapes=[float_vmem(outer_size, sketch_rows // row_size, col_count)] * 4
        + [float_vmem(col_size, sketch_rows // row_size, col_count), float_vmem(stack, col_count)]
        + [float_vmem(outer_size, stack // row_size, col_count)] * 4
        + [
            float_vmem(row_size, 2 * systems, col_count),
            dma((2, outer_size)), dma((2, outer_size)), dma((2, outer_size)), dma((2, outer_size)),
            dma((bit_total, col_size)), dma((col_size,)),
            dma((bit_total + 1, row_size, col_size)), dma((row_size, col_size)), dma((outer_size,)),
            dma((row_size,)), dma((row_size,)), dma((col_size,)), dma((col_size,)),
        ],
        compiler_params=pltpu.CompilerParams(
            collective_id=1, has_side_effects=True, vmem_limit_bytes=48 * 1024 * 1024
        ),
    )(row_signs, sampled, matrix, right_sides)


def local(matrix, row_signs, sampled_rows, right_sides):
    sampled = sampled_rows.reshape(-1, 1)
    gram_matrix, first, norm = sketched_gram(row_signs.reshape(1, -1), sampled, matrix, right_sides)
    inverse = inverse_factor(gram_matrix)
    return lsqr(matrix, inverse, right_sides, first, norm)


def solution(mesh):
    in_specs = (P("rows", "cols"), P("rows"), P("rows", None), P(None, "rows"))
    out_specs = (P(None, "cols"), P(None, "rows"))
    return jax.shard_map(local, mesh=mesh, in_specs=in_specs, out_specs=out_specs, check_vma=False)
```

```python
import functools
import math

import jax
import jax.numpy as jnp
from jax import lax
from jax.experimental import pallas as pl
from jax.experimental.pallas import tpu as pltpu
from jax.sharding import PartitionSpec as P

ROUNDS = 2
BLOCK = 128
STRIP = 8

highest = lax.Precision.HIGHEST


def block_inverse(square, beside):
    size = square.shape[0]
    row_ids = lax.broadcasted_iota(jnp.int32, (size, size), 0)
    col_ids = lax.broadcasted_iota(jnp.int32, (size, size), 1)
    rest = square
    unit = jnp.where(row_ids == col_ids, 1.0, 0.0).astype(jnp.float32)
    finished = []
    for strip in range(size // STRIP):
        beside(strip)
        start = strip * STRIP
        height = size - start
        here = lax.broadcasted_iota(jnp.int32, (height, size), 0)
        columns = [
            jnp.broadcast_to(rest[:, start + k:start + k + 1], (height, size)) for k in range(STRIP)
        ]
        scale = jnp.ones((STRIP, size), jnp.float32)
        for k in range(STRIP):
            pivot = columns[k][k:k + 1, :]
            factors = jnp.where(here > k, columns[k] * (1.0 / pivot), 0.0)
            for later in range(k + 1, STRIP):
                columns[later] = columns[later] - factors * columns[later][k:k + 1, :]
            rest = rest - factors * rest[k:k + 1, :]
            unit = unit - factors * unit[k:k + 1, :]
            scale = jnp.where(here[:STRIP] == k, lax.rsqrt(pivot), scale)
        finished.append(unit[:STRIP] * scale)
        rest = rest[STRIP:]
        unit = unit[STRIP:]
    return jnp.concatenate(finished, axis=0)


def three_parts(values):
    top = values.astype(jnp.bfloat16)
    rest = values - top.astype(jnp.float32)
    middle = rest.astype(jnp.bfloat16)
    return top, middle, (rest - middle.astype(jnp.float32)).astype(jnp.bfloat16)


def inverse_factor_kernel(gram_ref, out_ref, left_ref, right_ref):
    order = out_ref.shape[1]
    blocks = order // BLOCK
    col_size, _, width = gram_ref.shape
    half = width // 2
    for col in range(col_size):
        for other in range(col_size):
            low, high = min(col, other), max(col, other)
            start = low * width + (half if col > other else 0)
            if col == other:
                out_ref[start:start + width, high * width:(high + 1) * width] = gram_ref[col, :width, :]
                continue
            place = width + half * ((col ^ other) - 1)
            out_ref[start:start + half, high * width:(high + 1) * width] = gram_ref[col, place:place + half, :]
            if col > other:
                out_ref[col * width:(col + 1) * width, other * width:(other + 1) * width] = jnp.zeros(
                    (width, width), jnp.float32
                )

    out_ref[order:, :] = jnp.zeros((BLOCK, order), jnp.float32)
    left_ref[...] = jnp.zeros(left_ref.shape, jnp.bfloat16)
    right_ref[...] = jnp.zeros(right_ref.shape, jnp.bfloat16)
    col_ids = lax.broadcasted_iota(jnp.int32, (BLOCK, order), 1)

    def step(block, carry):
        start = pl.multiple_of(block * BLOCK, BLOCK)
        own = pl.ds(start, BLOCK)
        square = out_ref[own, own] - jnp.dot(
            left_ref[own, :], right_ref[:, own], preferred_element_type=jnp.float32
        )

        def update(strip):
            strips = BLOCK // STRIP
            for slot in range(strip * (blocks - 1) // strips, (strip + 1) * (blocks - 1) // strips):
                rows = pl.ds(pl.multiple_of(jnp.minimum(block + slot, blocks) * BLOCK, BLOCK), BLOCK)
                reduction = jnp.dot(left_ref[rows, :], right_ref[...], preferred_element_type=jnp.float32)
                fresh = (col_ids >= start - BLOCK) & (col_ids < start)
                out_ref[rows, :] = jnp.where(fresh, 0.0, out_ref[rows, :]) - reduction

        inverse = block_inverse(square, update)
        rows_done = jnp.dot(
            inverse, out_ref[own, :], precision=highest, preferred_element_type=jnp.float32
        )
        wide_inverse = jnp.concatenate([inverse] * blocks, axis=1)
        rows_done = jnp.where((col_ids >= start) & (col_ids < start + BLOCK), wide_inverse, rows_done)
        top, middle, low = three_parts(rows_done)
        right_ref[...] = jnp.concatenate([top, middle, top, middle, low, top], axis=0)
        top, middle, low = three_parts(rows_done.T)
        left_ref[:order, :] = jnp.concatenate([top, top, middle, middle, top, low], axis=1)
        out_ref[own, :] = jnp.where(col_ids < start + BLOCK, rows_done, 0.0)
        return carry

    lax.fori_loop(0, blocks, step, 0)


def inverse_factor(gram_matrix):
    order = gram_matrix.shape[0] * gram_matrix.shape[2]
    return pl.pallas_call(
        inverse_factor_kernel,
        out_shape=jax.ShapeDtypeStruct((order + BLOCK, order), jnp.float32),
        in_specs=[pl.BlockSpec(memory_space=pltpu.VMEM)],
        out_specs=pl.BlockSpec(memory_space=pltpu.VMEM),
        scratch_shapes=[
            pltpu.VMEM((order + BLOCK, 6 * BLOCK), jnp.bfloat16),
            pltpu.VMEM((6 * BLOCK, order), jnp.bfloat16),
        ],
        compiler_params=pltpu.CompilerParams(vmem_limit_bytes=32 * 1024 * 1024),
    )(gram_matrix)


MESH = pl.DeviceIdType.MESH


def greet(axes):
    barrier = pltpu.get_barrier_semaphore()
    count = 0
    for axis in axes:
        size = lax.axis_size(axis)
        me = lax.axis_index(axis)
        for offset in range(1, size):
            pl.semaphore_signal(
                barrier, inc=1, device_id={axis: lax.rem(me + offset, size)}, device_id_type=MESH
            )
        count += size - 1
    pl.semaphore_wait(barrier, count)


def share_copy(axis, slots, send_sem, recv_sem, offset, incoming):
    size = lax.axis_size(axis)
    me = lax.axis_index(axis)
    peer = lax.rem(me + (size - offset if incoming else offset), size)
    slot = peer if incoming else me
    return pltpu.make_async_remote_copy(
        src_ref=slots.at[slot], dst_ref=slots.at[slot],
        send_sem=send_sem.at[offset - 1], recv_sem=recv_sem.at[slot],
        device_id={axis: peer}, device_id_type=MESH,
    )


def share_start(axis, value, slots, send_sem, recv_sem):
    slots[lax.axis_index(axis)] = value
    for offset in range(1, lax.axis_size(axis)):
        share_copy(axis, slots, send_sem, recv_sem, offset, False).start()


def share_finish(axis, slots, send_sem, recv_sem):
    for offset in range(1, lax.axis_size(axis)):
        share_copy(axis, slots, send_sem, recv_sem, offset, True).wait_recv()
    for offset in range(1, lax.axis_size(axis)):
        share_copy(axis, slots, send_sem, recv_sem, offset, False).wait_send()


def share(axis, value, slots, send_sem, recv_sem):
    share_start(axis, value, slots, send_sem, recv_sem)
    share_finish(axis, slots, send_sem, recv_sem)


def added(slots):
    total = slots[0]
    for slot in range(1, slots.shape[0]):
        total = total + slots[slot]
    return total


def backward_part(vectors, matrix_ref):
    systems = vectors.shape[0]
    squares = jnp.sum(vectors * vectors, axis=1, keepdims=True)
    product = jnp.dot(split_rows(vectors), matrix_ref[...], preferred_element_type=jnp.float32)
    return jnp.concatenate(
        [join_rows(product, systems), jnp.broadcast_to(squares, (systems, matrix_ref.shape[1]))], axis=0
    )


def split_rows(vectors):
    top = vectors.astype(jnp.bfloat16).astype(jnp.float32)
    rest = vectors - top
    middle = rest.astype(jnp.bfloat16).astype(jnp.float32)
    low = rest - middle
    return jnp.concatenate([top, middle, low, jnp.zeros_like(low)], axis=0).astype(jnp.bfloat16)


def join_rows(stacked, systems):
    return stacked[:systems] + stacked[systems:2 * systems] + stacked[2 * systems:3 * systems]


def lsqr_kernel(
    matrix_ref, inverse_ref, right_ref, first_ref, norm_ref, solution_ref, residual_ref,
    row_slots, col_slots, image_slots, norm_slots,
    row_send, row_recv, col_send, col_recv, image_send, image_recv, norm_send, norm_recv,
):
    systems = right_ref.shape[0]
    col_count = matrix_ref.shape[1]
    order = inverse_ref.shape[1]
    own = pl.ds(pl.multiple_of(lax.axis_index("cols") * col_count, col_count), col_count)
    greet(("rows", "cols"))

    def forward(own_part, turn):
        product = lax.dot_general(
            split_rows(own_part), matrix_ref[...], (((1,), (1,)), ((), ())),
            preferred_element_type=jnp.float32,
        )
        share("cols", join_rows(product, systems), image_slots.at[turn], image_send.at[turn], image_recv.at[turn])
        return added(image_slots.at[turn])

    def backward(vectors, turn):
        share("rows", backward_part(vectors, matrix_ref), row_slots.at[turn], row_send.at[turn], row_recv.at[turn])
        total = added(row_slots.at[turn])
        norm = jnp.sqrt(total[systems:, 0:1])
        share("cols", total[:systems] / norm, col_slots.at[turn], col_send.at[turn], col_recv.at[turn])
        whole = jnp.concatenate([col_slots[turn, slot] for slot in range(col_slots.shape[1])], axis=1)
        return norm, whole

    def solve_right(vectors):
        return lax.dot_general(
            vectors, inverse_ref[:order, :], (((1,), (1,)), ((), ())),
            precision=highest, preferred_element_type=jnp.float32,
        )

    def solve_left(vectors):
        return jnp.dot(vectors, inverse_ref[:order, own], precision=highest, preferred_element_type=jnp.float32)

    def norm_of(vectors):
        return jnp.sqrt(jnp.sum(vectors * vectors, axis=1, keepdims=True))

    right_sides = right_ref[...]
    beta_norm = norm_ref[:, 0:1]
    whole_vector = jnp.concatenate([first_ref[slot] for slot in range(first_ref.shape[0])], axis=1)
    left_unit = right_sides / beta_norm
    back_rest = solve_right(whole_vector)
    alpha_norm = norm_of(back_rest)
    right_unit = back_rest / alpha_norm
    moved = solve_left(right_unit)
    image = forward(moved, 0)
    search, search_image = moved, image
    coeffs = jnp.zeros_like(moved)
    coeffs_image = jnp.zeros_like(image)
    phibar = beta_norm
    rhobar = alpha_norm
    for iteration in range(ROUNDS):
        last = iteration == ROUNDS - 1
        forward_rest = image - alpha_norm * left_unit
        if last:
            squares = jnp.sum(forward_rest * forward_rest, axis=1, keepdims=True)
            share("rows", jnp.broadcast_to(squares, norm_slots.shape[1:]), norm_slots, norm_send, norm_recv)
            beta_norm = jnp.sqrt(added(norm_slots)[:, 0:1])
        else:
            beta_norm, whole_vector = backward(forward_rest, iteration)
        rho_total = jnp.sqrt(rhobar * rhobar + beta_norm * beta_norm)
        cosine = rhobar / rho_total
        sine_part = beta_norm / rho_total
        ratio = cosine * phibar / rho_total
        coeffs = coeffs + ratio * search
        coeffs_image = coeffs_image + ratio * search_image
        if last:
            break
        left_unit = forward_rest / beta_norm
        back_rest = solve_right(whole_vector) - beta_norm * right_unit
        alpha_norm = norm_of(back_rest)
        right_unit = back_rest / alpha_norm
        moved = solve_left(right_unit)
        image = forward(moved, iteration + 1)
        shrink = sine_part * alpha_norm / rho_total
        rhobar = -cosine * alpha_norm
        phibar = sine_part * phibar
        search = moved - shrink * search
        search_image = image - shrink * search_image
    solution_ref[...] = coeffs
    residual_ref[...] = right_sides - coeffs_image


def lsqr(matrix, inverse, right_sides, first, norm):
    row_count, col_count = matrix.shape
    systems = right_sides.shape[0]
    row_size, col_size = lax.axis_size("rows"), lax.axis_size("cols")
    vmem = pl.BlockSpec(memory_space=pltpu.VMEM)
    dma = pltpu.SemaphoreType.DMA
    return pl.pallas_call(
        lsqr_kernel,
        out_shape=(
            jax.ShapeDtypeStruct((systems, col_count), jnp.float32),
            jax.ShapeDtypeStruct((systems, row_count), jnp.float32),
        ),
        in_specs=[vmem] * 5,
        out_specs=(vmem, vmem),
        scratch_shapes=[
            pltpu.VMEM((ROUNDS - 1, row_size, 2 * systems, col_count), jnp.float32),
            pltpu.VMEM((ROUNDS - 1, col_size, systems, col_count), jnp.float32),
            pltpu.VMEM((ROUNDS, col_size, systems, row_count), jnp.float32),
            pltpu.VMEM((row_size, systems, 128), jnp.float32),
            dma((ROUNDS - 1, row_size)), dma((ROUNDS - 1, row_size)),
            dma((ROUNDS - 1, col_size)), dma((ROUNDS - 1, col_size)),
            dma((ROUNDS, col_size)), dma((ROUNDS, col_size)),
            dma((row_size,)), dma((row_size,)),
        ],
        compiler_params=pltpu.CompilerParams(
            collective_id=0, has_side_effects=True, vmem_limit_bytes=40 * 1024 * 1024
        ),
    )(matrix, inverse, right_sides, first, norm)


def picked_mixer(sampled, signs):
    row_count = signs.shape[1]
    count = sampled.shape[0]
    lanes = min(128, row_count)
    common = sampled & lax.broadcasted_iota(jnp.int32, (count, lanes), 1)
    for shift in (4, 2, 1):
        common = common ^ lax.shift_right_logical(common, shift)
    mixer = jnp.where((common & 1) == 0, 1.0, -1.0).astype(jnp.float32)
    width = lanes
    while width < row_count:
        sign = jnp.where((sampled & width) == 0, 1.0, -1.0).astype(jnp.float32)
        mixer = jnp.concatenate([mixer, mixer * sign], axis=1)
        width = 2 * width
    return (mixer * signs).astype(jnp.bfloat16)


def col_bits(size):
    return [1 << place for place in range(size.bit_length() - 2, -1, -1)]


def gram_kernel(
    signs_ref, sampled_ref, matrix_ref, right_ref, gram_ref, first_ref, norm_ref,
    sketch_out, sketch_near, sketch_sum, sketch_far, pieces, partial,
    gram_out, gram_near, gram_sum, gram_far, row_slots,
    near_send, near_recv, far_send, far_recv, piece_send, piece_recv,
    block_send, block_recv, block_far_send, row_send, row_recv, col_send, col_recv,
):
    row_size, col_size = lax.axis_size("rows"), lax.axis_size("cols")
    row, col = lax.axis_index("rows"), lax.axis_index("cols")
    inner_size = 2 if row_size % 2 == 0 else 1
    outer_size = row_size // inner_size
    inner, outer = lax.rem(row, inner_size), row // inner_size
    col_count = matrix_ref.shape[1]
    sketch_rows = sampled_ref.shape[0]
    systems = right_ref.shape[0]
    bits = col_bits(col_size)
    started = []

    def flip(place, bit):
        return place + bit - 2 * bit * lax.rem(place // bit, 2)

    def start(source, target, send_sem, recv_sem, device):
        copy = pltpu.make_async_remote_copy(
            src_ref=source, dst_ref=target, send_sem=send_sem, recv_sem=recv_sem,
            device_id=device, device_id_type=MESH,
        )
        copy.start()
        started.append(copy)

    def arrived(target, recv_sem, device):
        pltpu.make_async_remote_copy(
            src_ref=target, dst_ref=target, send_sem=recv_sem, recv_sem=recv_sem,
            device_id=device, device_id_type=MESH,
        ).wait_recv()

    near_peer = {"rows": outer * inner_size + (inner_size - 1 - inner)}
    outer_order = [lax.rem(outer + step, outer_size) for step in range(1, outer_size)] + [outer]

    def reduce_scatter(turn, chunk, out, near, summed, far):
        if inner_size == 2:
            for other in outer_order:
                out[other] = chunk(other * inner_size + 1 - inner)
                start(out.at[other], near.at[other], near_send.at[turn, other], near_recv.at[turn, other], near_peer)
        total = None
        for step, other in enumerate(outer_order):
            total = chunk(other * inner_size + inner)
            if inner_size == 2:
                arrived(near.at[other], near_recv.at[turn, other], near_peer)
                total = total + near[other]
            if step < outer_size - 1:
                summed[other] = total
                start(
                    summed.at[other], far.at[outer], far_send.at[turn, other], far_recv.at[turn, outer],
                    {"rows": other * inner_size + inner},
                )
        for offset in range(1, outer_size):
            source = lax.rem(outer + outer_size - offset, outer_size)
            arrived(far.at[source], far_recv.at[turn, source], {"rows": source * inner_size + inner})
            total = total + far[source]
        return total

    greet(("rows", "cols"))

    share_start("rows", backward_part(right_ref[...], matrix_ref), row_slots, row_send, row_recv)

    piece_rows = sketch_rows // row_size

    signs = (1 - 2 * signs_ref[...]).astype(jnp.float32)

    def sketch_chunk(target):
        sampled = sampled_ref[pl.ds(pl.multiple_of(target * piece_rows, piece_rows), piece_rows), :]
        return jnp.dot(
            picked_mixer(sampled, signs), matrix_ref[...], preferred_element_type=jnp.float32
        ) * (1.0 / math.sqrt(sketch_rows))

    own_piece = reduce_scatter(0, sketch_chunk, sketch_out, sketch_near, sketch_sum, sketch_far)
    pieces[col] = own_piece
    for place, bit in enumerate(bits):
        start(pieces.at[col], pieces.at[col], piece_send.at[place, col], piece_recv.at[col], {"cols": flip(col, bit)})

    share_finish("rows", row_slots, row_send, row_recv)
    first_total = added(row_slots)
    first_norm = jnp.sqrt(first_total[systems:])
    norm_ref[...] = first_norm[:, :norm_ref.shape[1]]
    share_start("cols", first_total[:systems] / first_norm, first_ref, col_send, col_recv)

    masks = sorted(range(1, col_size), key=lambda mask: (-(mask & -mask), mask))

    def other_col(mask):
        place = col
        for bit in bits:
            if mask & bit:
                place = flip(place, bit)
        return place

    half = col_count // 2

    def product(left, right):
        return lax.dot_general(
            left, right, (((0,), (0,)), ((), ())), precision=highest, preferred_element_type=jnp.float32
        )

    def multiply(mask, block):
        top = 1 << (mask.bit_length() - 1)
        upper = lax.rem(col // top, 2)
        low = col - upper * (col - block)
        high = col + block - low
        place = col_count + half * (mask - 1)
        partial[place:place + half, :] = product(
            pieces[low, :, pl.ds(pl.multiple_of(upper * half, half), half)], pieces[high]
        )

    partial[:col_count, :] = product(own_piece, own_piece)
    used = col_count + half * (col_size - 1)
    if used < partial.shape[0]:
        partial[used:, :] = jnp.zeros((partial.shape[0] - used, col_count), jnp.float32)
    for mask in masks:
        block = other_col(mask)
        arrived(pieces.at[block], piece_recv.at[block], {"cols": flip(col, mask & -mask)})
        for place, bit in enumerate(bits):
            if bit < (mask & -mask):
                start(
                    pieces.at[block], pieces.at[block], piece_send.at[place, block], piece_recv.at[block],
                    {"cols": flip(col, bit)},
                )
        multiply(mask, block)

    block_rows = gram_ref.shape[1] // row_size

    def rows_of(target):
        return pl.ds(pl.multiple_of(target * block_rows, block_rows), block_rows)

    total = reduce_scatter(
        1, lambda target: partial[rows_of(target), :], gram_out, gram_near, gram_sum, gram_far
    )

    def block_ref(block_row, block_col):
        return gram_ref.at[block_col, rows_of(block_row), :]

    def pass_on(block_row, block_col, below):
        for place, bit in enumerate(bits):
            if bit < below:
                start(
                    block_ref(block_row, block_col), block_ref(block_row, block_col),
                    block_send.at[place, block_row, block_col], block_recv.at[block_row, block_col],
                    {"cols": flip(col, bit)},
                )

    def pass_near(block_row):
        if inner_size == 2:
            start(
                block_ref(block_row, col), block_ref(block_row, col),
                block_send.at[len(bits), block_row, col], block_recv.at[block_row, col], near_peer,
            )

    gram_ref[col, rows_of(row), :] = total
    for offset in range(1, outer_size):
        other = lax.rem(outer + offset, outer_size)
        start(
            block_ref(row, col), block_ref(row, col), block_far_send.at[offset], block_recv.at[row, col],
            {"rows": other * inner_size + inner},
        )
    pass_near(row)
    pass_on(row, col, col_size)
    for offset in range(1, outer_size):
        source = lax.rem(outer + outer_size - offset, outer_size) * inner_size + inner
        arrived(block_ref(source, col), block_recv.at[source, col], {"rows": source})
        pass_near(source)
        pass_on(source, col, col_size)
    by_distance = [lax.rem(outer + outer_size - offset, outer_size) for offset in range(outer_size)]
    if inner_size == 2:
        for other in by_distance:
            source = other * inner_size + 1 - inner
            arrived(block_ref(source, col), block_recv.at[source, col], near_peer)
            pass_on(source, col, col_size)
    for mask in masks:
        block = other_col(mask)
        for layer in range(inner_size):
            for other in by_distance:
                source = other * inner_size + (inner if layer == 0 else 1 - inner)
                arrived(block_ref(source, block), block_recv.at[source, block], {"cols": flip(col, mask & -mask)})
                pass_on(source, block, mask & -mask)
    share_finish("cols", first_ref, col_send, col_recv)
    for copy in started:
        copy.wait_send()


def sketched_gram(row_signs, sampled, matrix, right_sides):
    row_count, col_count = matrix.shape
    systems = right_sides.shape[0]
    sketch_rows = sampled.shape[0]
    row_size, col_size = lax.axis_size("rows"), lax.axis_size("cols")
    inner_size = 2 if row_size % 2 == 0 else 1
    outer_size = row_size // inner_size
    used = col_count + col_count // 2 * (col_size - 1)
    stack = row_size * STRIP * pl.cdiv(used, row_size * STRIP)
    bit_total = max(len(col_bits(col_size)), 1)
    vmem = pl.BlockSpec(memory_space=pltpu.VMEM)
    dma = pltpu.SemaphoreType.DMA
    float_vmem = lambda *shape: pltpu.VMEM(shape, jnp.float32)
    return pl.pallas_call(
        gram_kernel,
        out_shape=(
            jax.ShapeDtypeStruct((col_size, stack, col_count), jnp.float32),
            jax.ShapeDtypeStruct((col_size, systems, col_count), jnp.float32),
            jax.ShapeDtypeStruct((systems, 128), jnp.float32),
        ),
        in_specs=[vmem] * 4,
        out_specs=(vmem, vmem, vmem),
        scratch_shapes=[float_vmem(outer_size, sketch_rows // row_size, col_count)] * 4
        + [float_vmem(col_size, sketch_rows // row_size, col_count), float_vmem(stack, col_count)]
        + [float_vmem(outer_size, stack // row_size, col_count)] * 4
        + [
            float_vmem(row_size, 2 * systems, col_count),
            dma((2, outer_size)), dma((2, outer_size)), dma((2, outer_size)), dma((2, outer_size)),
            dma((bit_total, col_size)), dma((col_size,)),
            dma((bit_total + 1, row_size, col_size)), dma((row_size, col_size)), dma((outer_size,)),
            dma((row_size,)), dma((row_size,)), dma((col_size,)), dma((col_size,)),
        ],
        compiler_params=pltpu.CompilerParams(
            collective_id=1, has_side_effects=True, vmem_limit_bytes=48 * 1024 * 1024
        ),
    )(row_signs, sampled, matrix, right_sides)


def local(matrix, row_signs, sampled_rows, right_sides):
    sampled = sampled_rows.reshape(-1, 1)
    gram_matrix, first, norm = sketched_gram(row_signs.reshape(1, -1), sampled, matrix, right_sides)
    inverse = inverse_factor(gram_matrix)
    return lsqr(matrix, inverse, right_sides, first, norm)


def solution(mesh):
    in_specs = (P("rows", "cols"), P("rows"), P("rows", None), P(None, "rows"))
    out_specs = (P(None, "cols"), P(None, "rows"))
    return jax.shard_map(local, mesh=mesh, in_specs=in_specs, out_specs=out_specs, check_vma=False)
```

```python
import functools
import math

import jax
import jax.numpy as jnp
from jax import lax
from jax.experimental import pallas as pl
from jax.experimental.pallas import tpu as pltpu
from jax.sharding import PartitionSpec as P

ROUNDS = 2
BLOCK = 128
STRIP = 8

highest = lax.Precision.HIGHEST


def block_inverse(square, beside):
    size = square.shape[0]
    row_ids = lax.broadcasted_iota(jnp.int32, (size, size), 0)
    col_ids = lax.broadcasted_iota(jnp.int32, (size, size), 1)
    rest = square
    unit = jnp.where(row_ids == col_ids, 1.0, 0.0).astype(jnp.float32)
    finished = []
    for strip in range(size // STRIP):
        beside(strip)
        start = strip * STRIP
        height = size - start
        here = lax.broadcasted_iota(jnp.int32, (height, size), 0)
        columns = [
            jnp.broadcast_to(rest[:, start + k:start + k + 1], (height, size)) for k in range(STRIP)
        ]
        scale = jnp.ones((STRIP, size), jnp.float32)
        for k in range(STRIP):
            pivot = columns[k][k:k + 1, :]
            factors = jnp.where(here > k, columns[k] * (1.0 / pivot), 0.0)
            for later in range(k + 1, STRIP):
                columns[later] = columns[later] - factors * columns[later][k:k + 1, :]
            rest = rest - factors * rest[k:k + 1, :]
            unit = unit - factors * unit[k:k + 1, :]
            scale = jnp.where(here[:STRIP] == k, lax.rsqrt(pivot), scale)
        finished.append(unit[:STRIP] * scale)
        rest = rest[STRIP:]
        unit = unit[STRIP:]
    return jnp.concatenate(finished, axis=0)


def three_parts(values):
    top = values.astype(jnp.bfloat16)
    rest = values - top.astype(jnp.float32)
    middle = rest.astype(jnp.bfloat16)
    return top, middle, (rest - middle.astype(jnp.float32)).astype(jnp.bfloat16)


def inverse_factor_kernel(gram_ref, out_ref, inverse_ref, left_ref, right_ref):
    order = out_ref.shape[1]
    blocks = order // BLOCK
    col_size, _, width = gram_ref.shape
    half = width // 2
    for col in range(col_size):
        for other in range(col_size):
            low, high = min(col, other), max(col, other)
            start = low * width + (half if col > other else 0)
            if col == other:
                out_ref[start:start + width, high * width:(high + 1) * width] = gram_ref[col, :width, :]
                continue
            place = width + half * ((col ^ other) - 1)
            out_ref[start:start + half, high * width:(high + 1) * width] = gram_ref[col, place:place + half, :]
            if col > other:
                out_ref[col * width:(col + 1) * width, other * width:(other + 1) * width] = jnp.zeros(
                    (width, width), jnp.float32
                )

    out_ref[order:, :] = jnp.zeros((BLOCK, order), jnp.float32)
    left_ref[order:, :] = jnp.zeros((BLOCK, left_ref.shape[1]), jnp.bfloat16)
    inverse_ref[...] = jnp.zeros((BLOCK, BLOCK), jnp.float32)
    col_ids = lax.broadcasted_iota(jnp.int32, (BLOCK, order), 1)

    def times(left, right, contract):
        return lax.dot_general(
            left, right, (((contract,), (0,)), ((), ())), precision=highest, preferred_element_type=jnp.float32
        )

    def finish(rows, start):
        inverse = inverse_ref[...]
        done = times(inverse, out_ref[rows, :], 1)
        fresh = (col_ids >= start) & (col_ids < start + BLOCK)
        done = jnp.where(fresh, jnp.concatenate([inverse] * blocks, axis=1), done)
        out_ref[rows, :] = jnp.where(col_ids < start + BLOCK, done, 0.0)
        return done

    def step(block, carry):
        start = pl.multiple_of(block * BLOCK, BLOCK)
        own = pl.ds(start, BLOCK)
        before = pl.ds(pl.multiple_of(lax.rem(block + blocks, blocks + 1) * BLOCK, BLOCK), BLOCK)
        strip_part = times(inverse_ref[...], out_ref[before, own], 1)
        square = out_ref[own, own] - times(strip_part, strip_part, 0)

        def beside(strip):
            strips = BLOCK // STRIP
            if strip == 0:
                done = finish(before, start - BLOCK)
                top, middle, low = three_parts(done)
                right_ref[...] = jnp.concatenate([top, middle, top, middle, low, top], axis=0)
                top, middle, low = three_parts(done.T)
                left_ref[:order, :] = jnp.concatenate([top, top, middle, middle, top, low], axis=1)
            for slot in range(strip * (blocks - 1) // strips, (strip + 1) * (blocks - 1) // strips):
                rows = pl.ds(pl.multiple_of(jnp.minimum(block + slot, blocks) * BLOCK, BLOCK), BLOCK)
                reduction = jnp.dot(left_ref[rows, :], right_ref[...], preferred_element_type=jnp.float32)
                fresh = (col_ids >= start - BLOCK) & (col_ids < start)
                out_ref[rows, :] = jnp.where(fresh, 0.0, out_ref[rows, :]) - reduction

        inverse = block_inverse(square, beside)
        inverse_ref[...] = inverse
        return carry

    lax.fori_loop(0, blocks, step, 0)
    finish(pl.ds(order - BLOCK, BLOCK), order - BLOCK)


def inverse_factor(gram_matrix):
    order = gram_matrix.shape[0] * gram_matrix.shape[2]
    return pl.pallas_call(
        inverse_factor_kernel,
        out_shape=jax.ShapeDtypeStruct((order + BLOCK, order), jnp.float32),
        in_specs=[pl.BlockSpec(memory_space=pltpu.VMEM)],
        out_specs=pl.BlockSpec(memory_space=pltpu.VMEM),
        scratch_shapes=[
            pltpu.VMEM((BLOCK, BLOCK), jnp.float32),
            pltpu.VMEM((order + BLOCK, 6 * BLOCK), jnp.bfloat16),
            pltpu.VMEM((6 * BLOCK, order), jnp.bfloat16),
        ],
        compiler_params=pltpu.CompilerParams(vmem_limit_bytes=32 * 1024 * 1024),
    )(gram_matrix)


MESH = pl.DeviceIdType.MESH


def greet(axes):
    barrier = pltpu.get_barrier_semaphore()
    count = 0
    for axis in axes:
        size = lax.axis_size(axis)
        me = lax.axis_index(axis)
        for offset in range(1, size):
            pl.semaphore_signal(
                barrier, inc=1, device_id={axis: lax.rem(me + offset, size)}, device_id_type=MESH
            )
        count += size - 1
    pl.semaphore_wait(barrier, count)


def share_copy(axis, slots, send_sem, recv_sem, offset, incoming):
    size = lax.axis_size(axis)
    me = lax.axis_index(axis)
    peer = lax.rem(me + (size - offset if incoming else offset), size)
    slot = peer if incoming else me
    return pltpu.make_async_remote_copy(
        src_ref=slots.at[slot], dst_ref=slots.at[slot],
        send_sem=send_sem.at[offset - 1], recv_sem=recv_sem.at[slot],
        device_id={axis: peer}, device_id_type=MESH,
    )


def share_start(axis, value, slots, send_sem, recv_sem):
    slots[lax.axis_index(axis)] = value
    for offset in range(1, lax.axis_size(axis)):
        share_copy(axis, slots, send_sem, recv_sem, offset, False).start()


def share_finish(axis, slots, send_sem, recv_sem):
    for offset in range(1, lax.axis_size(axis)):
        share_copy(axis, slots, send_sem, recv_sem, offset, True).wait_recv()
    for offset in range(1, lax.axis_size(axis)):
        share_copy(axis, slots, send_sem, recv_sem, offset, False).wait_send()


def share(axis, value, slots, send_sem, recv_sem):
    share_start(axis, value, slots, send_sem, recv_sem)
    share_finish(axis, slots, send_sem, recv_sem)


def added(slots):
    total = slots[0]
    for slot in range(1, slots.shape[0]):
        total = total + slots[slot]
    return total


def backward_part(vectors, matrix_ref):
    systems = vectors.shape[0]
    squares = jnp.sum(vectors * vectors, axis=1, keepdims=True)
    product = jnp.dot(split_rows(vectors), matrix_ref[...], preferred_element_type=jnp.float32)
    return jnp.concatenate(
        [join_rows(product, systems), jnp.broadcast_to(squares, (systems, matrix_ref.shape[1]))], axis=0
    )


def split_rows(vectors):
    top = vectors.astype(jnp.bfloat16).astype(jnp.float32)
    rest = vectors - top
    middle = rest.astype(jnp.bfloat16).astype(jnp.float32)
    low = rest - middle
    return jnp.concatenate([top, middle, low, jnp.zeros_like(low)], axis=0).astype(jnp.bfloat16)


def join_rows(stacked, systems):
    return stacked[:systems] + stacked[systems:2 * systems] + stacked[2 * systems:3 * systems]


def lsqr_kernel(
    matrix_ref, inverse_ref, right_ref, first_ref, norm_ref, solution_ref, residual_ref,
    row_slots, col_slots, image_slots, norm_slots,
    row_send, row_recv, col_send, col_recv, image_send, image_recv, norm_send, norm_recv,
):
    systems = right_ref.shape[0]
    col_count = matrix_ref.shape[1]
    order = inverse_ref.shape[1]
    own = pl.ds(pl.multiple_of(lax.axis_index("cols") * col_count, col_count), col_count)
    greet(("rows", "cols"))

    def forward(own_part, turn):
        product = lax.dot_general(
            split_rows(own_part), matrix_ref[...], (((1,), (1,)), ((), ())),
            preferred_element_type=jnp.float32,
        )
        share("cols", join_rows(product, systems), image_slots.at[turn], image_send.at[turn], image_recv.at[turn])
        return added(image_slots.at[turn])

    def backward(vectors, turn):
        share("rows", backward_part(vectors, matrix_ref), row_slots.at[turn], row_send.at[turn], row_recv.at[turn])
        total = added(row_slots.at[turn])
        norm = jnp.sqrt(total[systems:, 0:1])
        share("cols", total[:systems] / norm, col_slots.at[turn], col_send.at[turn], col_recv.at[turn])
        whole = jnp.concatenate([col_slots[turn, slot] for slot in range(col_slots.shape[1])], axis=1)
        return norm, whole

    def solve_right(vectors):
        return lax.dot_general(
            vectors, inverse_ref[:order, :], (((1,), (1,)), ((), ())),
            precision=highest, preferred_element_type=jnp.float32,
        )

    def solve_left(vectors):
        return jnp.dot(vectors, inverse_ref[:order, own], precision=highest, preferred_element_type=jnp.float32)

    def norm_of(vectors):
        return jnp.sqrt(jnp.sum(vectors * vectors, axis=1, keepdims=True))

    right_sides = right_ref[...]
    beta_norm = norm_ref[:, 0:1]
    whole_vector = jnp.concatenate([first_ref[slot] for slot in range(first_ref.shape[0])], axis=1)
    left_unit = right_sides / beta_norm
    back_rest = solve_right(whole_vector)
    alpha_norm = norm_of(back_rest)
    right_unit = back_rest / alpha_norm
    moved = solve_left(right_unit)
    image = forward(moved, 0)
    search, search_image = moved, image
    coeffs = jnp.zeros_like(moved)
    coeffs_image = jnp.zeros_like(image)
    phibar = beta_norm
    rhobar = alpha_norm
    for iteration in range(ROUNDS):
        last = iteration == ROUNDS - 1
        forward_rest = image - alpha_norm * left_unit
        if last:
            squares = jnp.sum(forward_rest * forward_rest, axis=1, keepdims=True)
            share("rows", jnp.broadcast_to(squares, norm_slots.shape[1:]), norm_slots, norm_send, norm_recv)
            beta_norm = jnp.sqrt(added(norm_slots)[:, 0:1])
        else:
            beta_norm, whole_vector = backward(forward_rest, iteration)
        rho_total = jnp.sqrt(rhobar * rhobar + beta_norm * beta_norm)
        cosine = rhobar / rho_total
        sine_part = beta_norm / rho_total
        ratio = cosine * phibar / rho_total
        coeffs = coeffs + ratio * search
        coeffs_image = coeffs_image + ratio * search_image
        if last:
            break
        left_unit = forward_rest / beta_norm
        back_rest = solve_right(whole_vector) - beta_norm * right_unit
        alpha_norm = norm_of(back_rest)
        right_unit = back_rest / alpha_norm
        moved = solve_left(right_unit)
        image = forward(moved, iteration + 1)
        shrink = sine_part * alpha_norm / rho_total
        rhobar = -cosine * alpha_norm
        phibar = sine_part * phibar
        search = moved - shrink * search
        search_image = image - shrink * search_image
    solution_ref[...] = coeffs
    residual_ref[...] = right_sides - coeffs_image


def lsqr(matrix, inverse, right_sides, first, norm):
    row_count, col_count = matrix.shape
    systems = right_sides.shape[0]
    row_size, col_size = lax.axis_size("rows"), lax.axis_size("cols")
    vmem = pl.BlockSpec(memory_space=pltpu.VMEM)
    dma = pltpu.SemaphoreType.DMA
    return pl.pallas_call(
        lsqr_kernel,
        out_shape=(
            jax.ShapeDtypeStruct((systems, col_count), jnp.float32),
            jax.ShapeDtypeStruct((systems, row_count), jnp.float32),
        ),
        in_specs=[vmem] * 5,
        out_specs=(vmem, vmem),
        scratch_shapes=[
            pltpu.VMEM((ROUNDS - 1, row_size, 2 * systems, col_count), jnp.float32),
            pltpu.VMEM((ROUNDS - 1, col_size, systems, col_count), jnp.float32),
            pltpu.VMEM((ROUNDS, col_size, systems, row_count), jnp.float32),
            pltpu.VMEM((row_size, systems, 128), jnp.float32),
            dma((ROUNDS - 1, row_size)), dma((ROUNDS - 1, row_size)),
            dma((ROUNDS - 1, col_size)), dma((ROUNDS - 1, col_size)),
            dma((ROUNDS, col_size)), dma((ROUNDS, col_size)),
            dma((row_size,)), dma((row_size,)),
        ],
        compiler_params=pltpu.CompilerParams(
            collective_id=0, has_side_effects=True, vmem_limit_bytes=40 * 1024 * 1024
        ),
    )(matrix, inverse, right_sides, first, norm)


def picked_mixer(sampled, signs):
    row_count = signs.shape[1]
    count = sampled.shape[1]
    lanes = min(128, row_count)
    wide = jnp.broadcast_to(sampled, (lanes, count)).T
    common = wide & lax.broadcasted_iota(jnp.int32, (count, lanes), 1)
    for shift in (4, 2, 1):
        common = common ^ lax.shift_right_logical(common, shift)
    mixer = jnp.where((common & 1) == 0, 1.0, -1.0).astype(jnp.float32)
    width = lanes
    while width < row_count:
        sign = jnp.where((wide & width) == 0, 1.0, -1.0).astype(jnp.float32)
        mixer = jnp.concatenate([mixer, mixer * jnp.concatenate([sign] * (width // lanes), axis=1)], axis=1)
        width = 2 * width
    return (mixer * signs).astype(jnp.bfloat16)


def col_bits(size):
    return [1 << place for place in range(size.bit_length() - 2, -1, -1)]


def gram_kernel(
    signs_ref, sampled_ref, matrix_ref, right_ref, gram_ref, first_ref, norm_ref,
    sketch_out, sketch_near, sketch_sum, sketch_far, pieces, partial,
    gram_out, gram_near, gram_sum, gram_far, row_slots,
    near_send, near_recv, far_send, far_recv, piece_send, piece_recv,
    block_send, block_recv, block_far_send, row_send, row_recv, col_send, col_recv,
):
    row_size, col_size = lax.axis_size("rows"), lax.axis_size("cols")
    row, col = lax.axis_index("rows"), lax.axis_index("cols")
    inner_size = 2 if row_size % 2 == 0 else 1
    outer_size = row_size // inner_size
    inner, outer = lax.rem(row, inner_size), row // inner_size
    col_count = matrix_ref.shape[1]
    sketch_rows = sampled_ref.shape[0] * sampled_ref.shape[1]
    systems = right_ref.shape[0]
    bits = col_bits(col_size)
    started = []

    def flip(place, bit):
        return place + bit - 2 * bit * lax.rem(place // bit, 2)

    def start(source, target, send_sem, recv_sem, device):
        copy = pltpu.make_async_remote_copy(
            src_ref=source, dst_ref=target, send_sem=send_sem, recv_sem=recv_sem,
            device_id=device, device_id_type=MESH,
        )
        copy.start()
        started.append(copy)

    def arrived(target, recv_sem, device):
        pltpu.make_async_remote_copy(
            src_ref=target, dst_ref=target, send_sem=recv_sem, recv_sem=recv_sem,
            device_id=device, device_id_type=MESH,
        ).wait_recv()

    near_peer = {"rows": outer * inner_size + (inner_size - 1 - inner)}
    outer_order = [lax.rem(outer + step, outer_size) for step in range(1, outer_size)] + [outer]

    def reduce_scatter(turn, chunk, out, near, summed, far):
        if inner_size == 2:
            for other in outer_order:
                out[other] = chunk(other * inner_size + 1 - inner)
                start(out.at[other], near.at[other], near_send.at[turn, other], near_recv.at[turn, other], near_peer)
        total = None
        for step, other in enumerate(outer_order):
            total = chunk(other * inner_size + inner)
            if inner_size == 2:
                arrived(near.at[other], near_recv.at[turn, other], near_peer)
                total = total + near[other]
            if step < outer_size - 1:
                summed[other] = total
                start(
                    summed.at[other], far.at[outer], far_send.at[turn, other], far_recv.at[turn, outer],
                    {"rows": other * inner_size + inner},
                )
        for offset in range(1, outer_size):
            source = lax.rem(outer + outer_size - offset, outer_size)
            arrived(far.at[source], far_recv.at[turn, source], {"rows": source * inner_size + inner})
            total = total + far[source]
        return total

    greet(("rows", "cols"))

    share_start("rows", backward_part(right_ref[...], matrix_ref), row_slots, row_send, row_recv)

    signs = (1 - 2 * signs_ref[...]).astype(jnp.float32)

    def sketch_chunk(target):
        sampled = sampled_ref[pl.ds(target, 1), :]
        return jnp.dot(
            picked_mixer(sampled, signs), matrix_ref[...], preferred_element_type=jnp.float32
        ) * (1.0 / math.sqrt(sketch_rows))

    own_piece = reduce_scatter(0, sketch_chunk, sketch_out, sketch_near, sketch_sum, sketch_far)
    pieces[col] = own_piece
    for place, bit in enumerate(bits):
        start(pieces.at[col], pieces.at[col], piece_send.at[place, col], piece_recv.at[col], {"cols": flip(col, bit)})

    share_finish("rows", row_slots, row_send, row_recv)
    first_total = added(row_slots)
    first_norm = jnp.sqrt(first_total[systems:])
    norm_ref[...] = first_norm[:, :norm_ref.shape[1]]
    share_start("cols", first_total[:systems] / first_norm, first_ref, col_send, col_recv)

    masks = sorted(range(1, col_size), key=lambda mask: (-(mask & -mask), mask))

    def other_col(mask):
        place = col
        for bit in bits:
            if mask & bit:
                place = flip(place, bit)
        return place

    half = col_count // 2

    def product(left, right):
        return lax.dot_general(
            left, right, (((0,), (0,)), ((), ())), precision=highest, preferred_element_type=jnp.float32
        )

    def multiply(mask, block):
        top = 1 << (mask.bit_length() - 1)
        upper = lax.rem(col // top, 2)
        low = col - upper * (col - block)
        high = col + block - low
        place = col_count + half * (mask - 1)
        partial[place:place + half, :] = product(
            pieces[low, :, pl.ds(pl.multiple_of(upper * half, half), half)], pieces[high]
        )

    partial[:col_count, :] = product(own_piece, own_piece)
    used = col_count + half * (col_size - 1)
    if used < partial.shape[0]:
        partial[used:, :] = jnp.zeros((partial.shape[0] - used, col_count), jnp.float32)
    for mask in masks:
        block = other_col(mask)
        arrived(pieces.at[block], piece_recv.at[block], {"cols": flip(col, mask & -mask)})
        for place, bit in enumerate(bits):
            if bit < (mask & -mask):
                start(
                    pieces.at[block], pieces.at[block], piece_send.at[place, block], piece_recv.at[block],
                    {"cols": flip(col, bit)},
                )
        multiply(mask, block)

    block_rows = gram_ref.shape[1] // row_size

    def rows_of(target):
        return pl.ds(pl.multiple_of(target * block_rows, block_rows), block_rows)

    total = reduce_scatter(
        1, lambda target: partial[rows_of(target), :], gram_out, gram_near, gram_sum, gram_far
    )

    def block_ref(block_row, block_col):
        return gram_ref.at[block_col, rows_of(block_row), :]

    def pass_on(block_row, block_col, below):
        for place, bit in enumerate(bits):
            if bit < below:
                start(
                    block_ref(block_row, block_col), block_ref(block_row, block_col),
                    block_send.at[place, block_row, block_col], block_recv.at[block_row, block_col],
                    {"cols": flip(col, bit)},
                )

    def pass_near(block_row):
        if inner_size == 2:
            start(
                block_ref(block_row, col), block_ref(block_row, col),
                block_send.at[len(bits), block_row, col], block_recv.at[block_row, col], near_peer,
            )

    gram_ref[col, rows_of(row), :] = total
    for offset in range(1, outer_size):
        other = lax.rem(outer + offset, outer_size)
        start(
            block_ref(row, col), block_ref(row, col), block_far_send.at[offset], block_recv.at[row, col],
            {"rows": other * inner_size + inner},
        )
    pass_near(row)
    pass_on(row, col, col_size)
    for offset in range(1, outer_size):
        source = lax.rem(outer + outer_size - offset, outer_size) * inner_size + inner
        arrived(block_ref(source, col), block_recv.at[source, col], {"rows": source})
        pass_near(source)
        pass_on(source, col, col_size)
    by_distance = [lax.rem(outer + outer_size - offset, outer_size) for offset in range(outer_size)]
    if inner_size == 2:
        for other in by_distance:
            source = other * inner_size + 1 - inner
            arrived(block_ref(source, col), block_recv.at[source, col], near_peer)
            pass_on(source, col, col_size)
    for mask in masks:
        block = other_col(mask)
        for layer in range(inner_size):
            for other in by_distance:
                source = other * inner_size + (inner if layer == 0 else 1 - inner)
                arrived(block_ref(source, block), block_recv.at[source, block], {"cols": flip(col, mask & -mask)})
                pass_on(source, block, mask & -mask)
    share_finish("cols", first_ref, col_send, col_recv)
    for copy in started:
        copy.wait_send()


def sketched_gram(row_signs, sampled, matrix, right_sides):
    row_count, col_count = matrix.shape
    systems = right_sides.shape[0]
    sketch_rows = sampled.shape[0] * sampled.shape[1]
    row_size, col_size = lax.axis_size("rows"), lax.axis_size("cols")
    inner_size = 2 if row_size % 2 == 0 else 1
    outer_size = row_size // inner_size
    used = col_count + col_count // 2 * (col_size - 1)
    stack = row_size * STRIP * pl.cdiv(used, row_size * STRIP)
    bit_total = max(len(col_bits(col_size)), 1)
    vmem = pl.BlockSpec(memory_space=pltpu.VMEM)
    dma = pltpu.SemaphoreType.DMA
    float_vmem = lambda *shape: pltpu.VMEM(shape, jnp.float32)
    return pl.pallas_call(
        gram_kernel,
        out_shape=(
            jax.ShapeDtypeStruct((col_size, stack, col_count), jnp.float32),
            jax.ShapeDtypeStruct((col_size, systems, col_count), jnp.float32),
            jax.ShapeDtypeStruct((systems, 128), jnp.float32),
        ),
        in_specs=[vmem] * 4,
        out_specs=(vmem, vmem, vmem),
        scratch_shapes=[float_vmem(outer_size, sketch_rows // row_size, col_count)] * 4
        + [float_vmem(col_size, sketch_rows // row_size, col_count), float_vmem(stack, col_count)]
        + [float_vmem(outer_size, stack // row_size, col_count)] * 4
        + [
            float_vmem(row_size, 2 * systems, col_count),
            dma((2, outer_size)), dma((2, outer_size)), dma((2, outer_size)), dma((2, outer_size)),
            dma((bit_total, col_size)), dma((col_size,)),
            dma((bit_total + 1, row_size, col_size)), dma((row_size, col_size)), dma((outer_size,)),
            dma((row_size,)), dma((row_size,)), dma((col_size,)), dma((col_size,)),
        ],
        compiler_params=pltpu.CompilerParams(
            collective_id=1, has_side_effects=True, vmem_limit_bytes=48 * 1024 * 1024
        ),
    )(row_signs, sampled, matrix, right_sides)


def local(matrix, row_signs, sampled_rows, right_sides):
    sampled = sampled_rows.reshape(lax.axis_size("rows"), -1)
    gram_matrix, first, norm = sketched_gram(row_signs.reshape(1, -1), sampled, matrix, right_sides)
    inverse = inverse_factor(gram_matrix)
    return lsqr(matrix, inverse, right_sides, first, norm)


def solution(mesh):
    in_specs = (P("rows", "cols"), P("rows"), P("rows", None), P(None, "rows"))
    out_specs = (P(None, "cols"), P(None, "rows"))
    return jax.shard_map(local, mesh=mesh, in_specs=in_specs, out_specs=out_specs, check_vma=False)
```

```python
import functools
import math

import jax
import jax.numpy as jnp
from jax import lax
from jax.experimental import pallas as pl
from jax.experimental.pallas import tpu as pltpu
from jax.sharding import PartitionSpec as P

ROUNDS = 2
BLOCK = 128
STRIP = 8

highest = lax.Precision.HIGHEST


def block_inverse(square, beside):
    size = square.shape[0]
    row_ids = lax.broadcasted_iota(jnp.int32, (size, size), 0)
    col_ids = lax.broadcasted_iota(jnp.int32, (size, size), 1)
    rest = square
    unit = jnp.where(row_ids == col_ids, 1.0, 0.0).astype(jnp.float32)
    finished = []
    for strip in range(size // STRIP):
        beside(strip)
        start = strip * STRIP
        height = size - start
        here = lax.broadcasted_iota(jnp.int32, (height, size), 0)
        columns = [
            jnp.broadcast_to(rest[:, start + k:start + k + 1], (height, size)) for k in range(STRIP)
        ]
        scale = jnp.ones((STRIP, size), jnp.float32)
        for k in range(STRIP):
            pivot = columns[k][k:k + 1, :]
            factors = jnp.where(here > k, columns[k] * (1.0 / pivot), 0.0)
            for later in range(k + 1, STRIP):
                columns[later] = columns[later] - factors * columns[later][k:k + 1, :]
            rest = rest - factors * rest[k:k + 1, :]
            unit = unit - factors * unit[k:k + 1, :]
            scale = jnp.where(here[:STRIP] == k, lax.rsqrt(pivot), scale)
        finished.append(unit[:STRIP] * scale)
        rest = rest[STRIP:]
        unit = unit[STRIP:]
    return jnp.concatenate(finished, axis=0)


def three_parts(values):
    top = values.astype(jnp.bfloat16)
    rest = values - top.astype(jnp.float32)
    middle = rest.astype(jnp.bfloat16)
    return top, middle, (rest - middle.astype(jnp.float32)).astype(jnp.bfloat16)


def inverse_factor_kernel(gram_ref, out_ref, inverse_ref, left_ref, right_ref):
    order = out_ref.shape[1]
    blocks = order // BLOCK
    col_size, _, width = gram_ref.shape
    half = width // 2
    for col in range(col_size):
        for other in range(col_size):
            low, high = min(col, other), max(col, other)
            start = low * width + (half if col > other else 0)
            if col == other:
                out_ref[start:start + width, high * width:(high + 1) * width] = gram_ref[col, :width, :]
                continue
            place = width + half * ((col ^ other) - 1)
            out_ref[start:start + half, high * width:(high + 1) * width] = gram_ref[col, place:place + half, :]
            if col > other:
                out_ref[col * width:(col + 1) * width, other * width:(other + 1) * width] = jnp.zeros(
                    (width, width), jnp.float32
                )

    out_ref[order:, :] = jnp.zeros((BLOCK, order), jnp.float32)
    left_ref[order:, :] = jnp.zeros((BLOCK, left_ref.shape[1]), jnp.bfloat16)
    inverse_ref[...] = jnp.zeros((BLOCK, BLOCK), jnp.float32)
    col_ids = lax.broadcasted_iota(jnp.int32, (BLOCK, order), 1)

    def times(left, right, contract):
        return lax.dot_general(
            left, right, (((contract,), (0,)), ((), ())), precision=highest, preferred_element_type=jnp.float32
        )

    def finish(rows, start):
        inverse = inverse_ref[...]
        done = times(inverse, out_ref[rows, :], 1)
        fresh = (col_ids >= start) & (col_ids < start + BLOCK)
        done = jnp.where(fresh, jnp.concatenate([inverse] * blocks, axis=1), done)
        out_ref[rows, :] = jnp.where(col_ids < start + BLOCK, done, 0.0)
        return done

    def step(block, carry):
        start = pl.multiple_of(block * BLOCK, BLOCK)
        own = pl.ds(start, BLOCK)
        before = pl.ds(pl.multiple_of(lax.rem(block + blocks, blocks + 1) * BLOCK, BLOCK), BLOCK)
        strip_part = times(inverse_ref[...], out_ref[before, own], 1)
        square = out_ref[own, own] - times(strip_part, strip_part, 0)

        def beside(strip):
            strips = BLOCK // STRIP
            if strip == 0:
                done = finish(before, start - BLOCK)
                top, middle, low = three_parts(done)
                right_ref[...] = jnp.concatenate([top, middle, top, middle, low, top], axis=0)
                top, middle, low = three_parts(done.T)
                left_ref[:order, :] = jnp.concatenate([top, top, middle, middle, top, low], axis=1)
            for slot in range(strip * (blocks - 1) // strips, (strip + 1) * (blocks - 1) // strips):
                rows = pl.ds(pl.multiple_of(jnp.minimum(block + slot, blocks) * BLOCK, BLOCK), BLOCK)
                reduction = jnp.dot(left_ref[rows, :], right_ref[...], preferred_element_type=jnp.float32)
                fresh = (col_ids >= start - BLOCK) & (col_ids < start)
                out_ref[rows, :] = jnp.where(fresh, 0.0, out_ref[rows, :]) - reduction

        inverse = block_inverse(square, beside)
        inverse_ref[...] = inverse
        return carry

    lax.fori_loop(0, blocks, step, 0)
    finish(pl.ds(order - BLOCK, BLOCK), order - BLOCK)


def inverse_factor(gram_matrix):
    order = gram_matrix.shape[0] * gram_matrix.shape[2]
    return pl.pallas_call(
        inverse_factor_kernel,
        out_shape=jax.ShapeDtypeStruct((order + BLOCK, order), jnp.float32),
        in_specs=[pl.BlockSpec(memory_space=pltpu.VMEM)],
        out_specs=pl.BlockSpec(memory_space=pltpu.VMEM),
        scratch_shapes=[
            pltpu.VMEM((BLOCK, BLOCK), jnp.float32),
            pltpu.VMEM((order + BLOCK, 6 * BLOCK), jnp.bfloat16),
            pltpu.VMEM((6 * BLOCK, order), jnp.bfloat16),
        ],
        compiler_params=pltpu.CompilerParams(vmem_limit_bytes=32 * 1024 * 1024),
    )(gram_matrix)


MESH = pl.DeviceIdType.MESH


def greet(axes):
    barrier = pltpu.get_barrier_semaphore()
    count = 0
    for axis in axes:
        size = lax.axis_size(axis)
        me = lax.axis_index(axis)
        for offset in range(1, size):
            pl.semaphore_signal(
                barrier, inc=1, device_id={axis: lax.rem(me + offset, size)}, device_id_type=MESH
            )
        count += size - 1
    pl.semaphore_wait(barrier, count)


def share_copy(axis, slots, send_sem, recv_sem, offset, incoming):
    size = lax.axis_size(axis)
    me = lax.axis_index(axis)
    peer = lax.rem(me + (size - offset if incoming else offset), size)
    slot = peer if incoming else me
    return pltpu.make_async_remote_copy(
        src_ref=slots.at[slot], dst_ref=slots.at[slot],
        send_sem=send_sem.at[offset - 1], recv_sem=recv_sem.at[slot],
        device_id={axis: peer}, device_id_type=MESH,
    )


def share_start(axis, value, slots, send_sem, recv_sem):
    slots[lax.axis_index(axis)] = value
    for offset in range(1, lax.axis_size(axis)):
        share_copy(axis, slots, send_sem, recv_sem, offset, False).start()


def share_finish(axis, slots, send_sem, recv_sem):
    for offset in range(1, lax.axis_size(axis)):
        share_copy(axis, slots, send_sem, recv_sem, offset, True).wait_recv()
    for offset in range(1, lax.axis_size(axis)):
        share_copy(axis, slots, send_sem, recv_sem, offset, False).wait_send()


def share(axis, value, slots, send_sem, recv_sem):
    share_start(axis, value, slots, send_sem, recv_sem)
    share_finish(axis, slots, send_sem, recv_sem)


def added(slots):
    total = slots[0]
    for slot in range(1, slots.shape[0]):
        total = total + slots[slot]
    return total


def backward_part(vectors, matrix_ref):
    systems = vectors.shape[0]
    squares = jnp.sum(vectors * vectors, axis=1, keepdims=True)
    product = jnp.dot(split_rows(vectors), matrix_ref[...], preferred_element_type=jnp.float32)
    return jnp.concatenate(
        [join_rows(product, systems), jnp.broadcast_to(squares, (systems, matrix_ref.shape[1]))], axis=0
    )


def split_rows(vectors):
    top = vectors.astype(jnp.bfloat16).astype(jnp.float32)
    rest = vectors - top
    middle = rest.astype(jnp.bfloat16).astype(jnp.float32)
    low = rest - middle
    return jnp.concatenate([top, middle, low, jnp.zeros_like(low)], axis=0).astype(jnp.bfloat16)


def join_rows(stacked, systems):
    return stacked[:systems] + stacked[systems:2 * systems] + stacked[2 * systems:3 * systems]


def lsqr_kernel(
    matrix_ref, inverse_ref, right_ref, first_ref, norm_ref, solution_ref, residual_ref,
    row_slots, col_slots, image_slots, norm_slots,
    row_send, row_recv, col_send, col_recv, image_send, image_recv, norm_send, norm_recv,
):
    systems = right_ref.shape[0]
    col_count = matrix_ref.shape[1]
    order = inverse_ref.shape[1]
    own = pl.ds(pl.multiple_of(lax.axis_index("cols") * col_count, col_count), col_count)
    greet(("rows", "cols"))

    def forward(own_part, turn):
        product = lax.dot_general(
            split_rows(own_part), matrix_ref[...], (((1,), (1,)), ((), ())),
            preferred_element_type=jnp.float32,
        )
        share("cols", join_rows(product, systems), image_slots.at[turn], image_send.at[turn], image_recv.at[turn])
        return added(image_slots.at[turn])

    def backward(vectors, turn):
        share("rows", backward_part(vectors, matrix_ref), row_slots.at[turn], row_send.at[turn], row_recv.at[turn])
        total = added(row_slots.at[turn])
        norm = jnp.sqrt(total[systems:, 0:1])
        share("cols", total[:systems] / norm, col_slots.at[turn], col_send.at[turn], col_recv.at[turn])
        whole = jnp.concatenate([col_slots[turn, slot] for slot in range(col_slots.shape[1])], axis=1)
        return norm, whole

    def solve_right(vectors):
        return lax.dot_general(
            vectors, inverse_ref[:order, :], (((1,), (1,)), ((), ())),
            precision=highest, preferred_element_type=jnp.float32,
        )

    def solve_left(vectors):
        return jnp.dot(vectors, inverse_ref[:order, own], precision=highest, preferred_element_type=jnp.float32)

    def norm_of(vectors):
        return jnp.sqrt(jnp.sum(vectors * vectors, axis=1, keepdims=True))

    right_sides = right_ref[...]
    beta_norm = norm_ref[:, 0:1]
    whole_vector = jnp.concatenate([first_ref[slot] for slot in range(first_ref.shape[0])], axis=1)
    left_unit = right_sides / beta_norm
    back_rest = solve_right(whole_vector)
    alpha_norm = norm_of(back_rest)
    right_unit = back_rest / alpha_norm
    moved = solve_left(right_unit)
    image = forward(moved, 0)
    search, search_image = moved, image
    coeffs = jnp.zeros_like(moved)
    coeffs_image = jnp.zeros_like(image)
    phibar = beta_norm
    rhobar = alpha_norm
    for iteration in range(ROUNDS):
        last = iteration == ROUNDS - 1
        forward_rest = image - alpha_norm * left_unit
        if last:
            squares = jnp.sum(forward_rest * forward_rest, axis=1, keepdims=True)
            share("rows", jnp.broadcast_to(squares, norm_slots.shape[1:]), norm_slots, norm_send, norm_recv)
            beta_norm = jnp.sqrt(added(norm_slots)[:, 0:1])
        else:
            beta_norm, whole_vector = backward(forward_rest, iteration)
        rho_total = jnp.sqrt(rhobar * rhobar + beta_norm * beta_norm)
        cosine = rhobar / rho_total
        sine_part = beta_norm / rho_total
        ratio = cosine * phibar / rho_total
        coeffs = coeffs + ratio * search
        coeffs_image = coeffs_image + ratio * search_image
        if last:
            break
        left_unit = forward_rest / beta_norm
        back_rest = solve_right(whole_vector) - beta_norm * right_unit
        alpha_norm = norm_of(back_rest)
        right_unit = back_rest / alpha_norm
        moved = solve_left(right_unit)
        image = forward(moved, iteration + 1)
        shrink = sine_part * alpha_norm / rho_total
        rhobar = -cosine * alpha_norm
        phibar = sine_part * phibar
        search = moved - shrink * search
        search_image = image - shrink * search_image
    solution_ref[...] = coeffs
    residual_ref[...] = right_sides - coeffs_image


def lsqr(matrix, inverse, right_sides, first, norm):
    row_count, col_count = matrix.shape
    systems = right_sides.shape[0]
    row_size, col_size = lax.axis_size("rows"), lax.axis_size("cols")
    vmem = pl.BlockSpec(memory_space=pltpu.VMEM)
    dma = pltpu.SemaphoreType.DMA
    return pl.pallas_call(
        lsqr_kernel,
        out_shape=(
            jax.ShapeDtypeStruct((systems, col_count), jnp.float32),
            jax.ShapeDtypeStruct((systems, row_count), jnp.float32),
        ),
        in_specs=[vmem] * 5,
        out_specs=(vmem, vmem),
        scratch_shapes=[
            pltpu.VMEM((ROUNDS - 1, row_size, 2 * systems, col_count), jnp.float32),
            pltpu.VMEM((ROUNDS - 1, col_size, systems, col_count), jnp.float32),
            pltpu.VMEM((ROUNDS, col_size, systems, row_count), jnp.float32),
            pltpu.VMEM((row_size, systems, 128), jnp.float32),
            dma((ROUNDS - 1, row_size)), dma((ROUNDS - 1, row_size)),
            dma((ROUNDS - 1, col_size)), dma((ROUNDS - 1, col_size)),
            dma((ROUNDS, col_size)), dma((ROUNDS, col_size)),
            dma((row_size,)), dma((row_size,)),
        ],
        compiler_params=pltpu.CompilerParams(
            collective_id=0, has_side_effects=True, vmem_limit_bytes=40 * 1024 * 1024
        ),
    )(matrix, inverse, right_sides, first, norm)


def picked_mixer(sampled, signs):
    row_count = signs.shape[1]
    count = sampled.shape[1]
    lanes = min(128, row_count)
    wide = jnp.broadcast_to(sampled, (lanes, count)).T
    common = wide & lax.broadcasted_iota(jnp.int32, (count, lanes), 1)
    for shift in (4, 2, 1):
        common = common ^ lax.shift_right_logical(common, shift)
    mixer = jnp.where((common & 1) == 0, 1.0, -1.0).astype(jnp.float32)
    width = lanes
    while width < row_count:
        sign = jnp.where((wide & width) == 0, 1.0, -1.0).astype(jnp.float32)
        mixer = jnp.concatenate([mixer, mixer * jnp.concatenate([sign] * (width // lanes), axis=1)], axis=1)
        width = 2 * width
    return (mixer * signs).astype(jnp.bfloat16)


def col_bits(size):
    return [1 << place for place in range(size.bit_length() - 2, -1, -1)]


def gram_kernel(
    signs_ref, sampled_ref, matrix_ref, right_ref, gram_ref, first_ref, norm_ref,
    sketch_out, sketch_near, sketch_sum, sketch_far, pieces, partial,
    gram_out, gram_near, gram_sum, gram_far, row_slots,
    near_send, near_recv, far_send, far_recv, piece_send, piece_recv,
    block_send, block_recv, block_far_send, row_send, row_recv, col_send, col_recv,
):
    row_size, col_size = lax.axis_size("rows"), lax.axis_size("cols")
    row, col = lax.axis_index("rows"), lax.axis_index("cols")
    inner_size = 2 if row_size % 2 == 0 else 1
    outer_size = row_size // inner_size
    inner, outer = lax.rem(row, inner_size), row // inner_size
    col_count = matrix_ref.shape[1]
    sketch_rows = sampled_ref.shape[0] * sampled_ref.shape[1]
    systems = right_ref.shape[0]
    bits = col_bits(col_size)
    started = []

    def flip(place, bit):
        return place + bit - 2 * bit * lax.rem(place // bit, 2)

    def start(source, target, send_sem, recv_sem, device):
        copy = pltpu.make_async_remote_copy(
            src_ref=source, dst_ref=target, send_sem=send_sem, recv_sem=recv_sem,
            device_id=device, device_id_type=MESH,
        )
        copy.start()
        started.append(copy)

    def arrived(target, recv_sem, device):
        pltpu.make_async_remote_copy(
            src_ref=target, dst_ref=target, send_sem=recv_sem, recv_sem=recv_sem,
            device_id=device, device_id_type=MESH,
        ).wait_recv()

    near_peer = {"rows": outer * inner_size + (inner_size - 1 - inner)}
    outer_order = [lax.rem(outer + step, outer_size) for step in range(1, outer_size)] + [outer]

    def reduce_scatter(turn, chunk, out, near, summed, far):
        if inner_size == 2:
            for other in outer_order:
                out[other] = chunk(other * inner_size + 1 - inner)
                start(out.at[other], near.at[other], near_send.at[turn, other], near_recv.at[turn, other], near_peer)
        total = None
        for step, other in enumerate(outer_order):
            total = chunk(other * inner_size + inner)
            if inner_size == 2:
                arrived(near.at[other], near_recv.at[turn, other], near_peer)
                total = total + near[other]
            if step < outer_size - 1:
                summed[other] = total
                start(
                    summed.at[other], far.at[outer], far_send.at[turn, other], far_recv.at[turn, outer],
                    {"rows": other * inner_size + inner},
                )
        for offset in range(1, outer_size):
            source = lax.rem(outer + outer_size - offset, outer_size)
            arrived(far.at[source], far_recv.at[turn, source], {"rows": source * inner_size + inner})
            total = total + far[source]
        return total

    greet(("rows", "cols"))

    signs = (1 - 2 * signs_ref[...]).astype(jnp.float32)

    def sketch_chunk(target):
        sampled = sampled_ref[pl.ds(target, 1), :]
        return jnp.dot(
            picked_mixer(sampled, signs), matrix_ref[...], preferred_element_type=jnp.float32
        ) * (1.0 / math.sqrt(sketch_rows))

    own_piece = reduce_scatter(0, sketch_chunk, sketch_out, sketch_near, sketch_sum, sketch_far)
    pieces[col] = own_piece
    for place, bit in enumerate(bits):
        start(pieces.at[col], pieces.at[col], piece_send.at[place, col], piece_recv.at[col], {"cols": flip(col, bit)})

    share_start("rows", backward_part(right_ref[...], matrix_ref), row_slots, row_send, row_recv)

    masks = sorted(range(1, col_size), key=lambda mask: (-(mask & -mask), mask))

    def other_col(mask):
        place = col
        for bit in bits:
            if mask & bit:
                place = flip(place, bit)
        return place

    half = col_count // 2

    def product(left, right):
        return lax.dot_general(
            left, right, (((0,), (0,)), ((), ())), precision=highest, preferred_element_type=jnp.float32
        )

    def multiply(mask, block):
        top = 1 << (mask.bit_length() - 1)
        upper = lax.rem(col // top, 2)
        low = col - upper * (col - block)
        high = col + block - low
        place = col_count + half * (mask - 1)
        partial[place:place + half, :] = product(
            pieces[low, :, pl.ds(pl.multiple_of(upper * half, half), half)], pieces[high]
        )

    partial[:col_count, :] = product(own_piece, own_piece)
    used = col_count + half * (col_size - 1)
    if used < partial.shape[0]:
        partial[used:, :] = jnp.zeros((partial.shape[0] - used, col_count), jnp.float32)
    for mask in masks:
        block = other_col(mask)
        arrived(pieces.at[block], piece_recv.at[block], {"cols": flip(col, mask & -mask)})
        for place, bit in enumerate(bits):
            if bit < (mask & -mask):
                start(
                    pieces.at[block], pieces.at[block], piece_send.at[place, block], piece_recv.at[block],
                    {"cols": flip(col, bit)},
                )
        multiply(mask, block)

    share_finish("rows", row_slots, row_send, row_recv)
    first_total = added(row_slots)
    first_norm = jnp.sqrt(first_total[systems:])
    norm_ref[...] = first_norm[:, :norm_ref.shape[1]]
    share_start("cols", first_total[:systems] / first_norm, first_ref, col_send, col_recv)

    block_rows = gram_ref.shape[1] // row_size

    def rows_of(target):
        return pl.ds(pl.multiple_of(target * block_rows, block_rows), block_rows)

    total = reduce_scatter(
        1, lambda target: partial[rows_of(target), :], gram_out, gram_near, gram_sum, gram_far
    )

    def block_ref(block_row, block_col):
        return gram_ref.at[block_col, rows_of(block_row), :]

    def pass_on(block_row, block_col, below):
        for place, bit in enumerate(bits):
            if bit < below:
                start(
                    block_ref(block_row, block_col), block_ref(block_row, block_col),
                    block_send.at[place, block_row, block_col], block_recv.at[block_row, block_col],
                    {"cols": flip(col, bit)},
                )

    def pass_near(block_row):
        if inner_size == 2:
            start(
                block_ref(block_row, col), block_ref(block_row, col),
                block_send.at[len(bits), block_row, col], block_recv.at[block_row, col], near_peer,
            )

    gram_ref[col, rows_of(row), :] = total
    for offset in range(1, outer_size):
        other = lax.rem(outer + offset, outer_size)
        start(
            block_ref(row, col), block_ref(row, col), block_far_send.at[offset], block_recv.at[row, col],
            {"rows": other * inner_size + inner},
        )
    pass_near(row)
    pass_on(row, col, col_size)
    for offset in range(1, outer_size):
        source = lax.rem(outer + outer_size - offset, outer_size) * inner_size + inner
        arrived(block_ref(source, col), block_recv.at[source, col], {"rows": source})
        pass_near(source)
        pass_on(source, col, col_size)
    by_distance = [lax.rem(outer + outer_size - offset, outer_size) for offset in range(outer_size)]
    if inner_size == 2:
        for other in by_distance:
            source = other * inner_size + 1 - inner
            arrived(block_ref(source, col), block_recv.at[source, col], near_peer)
            pass_on(source, col, col_size)
    for mask in masks:
        block = other_col(mask)
        for layer in range(inner_size):
            for other in by_distance:
                source = other * inner_size + (inner if layer == 0 else 1 - inner)
                arrived(block_ref(source, block), block_recv.at[source, block], {"cols": flip(col, mask & -mask)})
                pass_on(source, block, mask & -mask)
    share_finish("cols", first_ref, col_send, col_recv)
    for copy in started:
        copy.wait_send()


def sketched_gram(row_signs, sampled, matrix, right_sides):
    row_count, col_count = matrix.shape
    systems = right_sides.shape[0]
    sketch_rows = sampled.shape[0] * sampled.shape[1]
    row_size, col_size = lax.axis_size("rows"), lax.axis_size("cols")
    inner_size = 2 if row_size % 2 == 0 else 1
    outer_size = row_size // inner_size
    used = col_count + col_count // 2 * (col_size - 1)
    stack = row_size * STRIP * pl.cdiv(used, row_size * STRIP)
    bit_total = max(len(col_bits(col_size)), 1)
    vmem = pl.BlockSpec(memory_space=pltpu.VMEM)
    dma = pltpu.SemaphoreType.DMA
    float_vmem = lambda *shape: pltpu.VMEM(shape, jnp.float32)
    return pl.pallas_call(
        gram_kernel,
        out_shape=(
            jax.ShapeDtypeStruct((col_size, stack, col_count), jnp.float32),
            jax.ShapeDtypeStruct((col_size, systems, col_count), jnp.float32),
            jax.ShapeDtypeStruct((systems, 128), jnp.float32),
        ),
        in_specs=[vmem] * 4,
        out_specs=(vmem, vmem, vmem),
        scratch_shapes=[float_vmem(outer_size, sketch_rows // row_size, col_count)] * 4
        + [float_vmem(col_size, sketch_rows // row_size, col_count), float_vmem(stack, col_count)]
        + [float_vmem(outer_size, stack // row_size, col_count)] * 4
        + [
            float_vmem(row_size, 2 * systems, col_count),
            dma((2, outer_size)), dma((2, outer_size)), dma((2, outer_size)), dma((2, outer_size)),
            dma((bit_total, col_size)), dma((col_size,)),
            dma((bit_total + 1, row_size, col_size)), dma((row_size, col_size)), dma((outer_size,)),
            dma((row_size,)), dma((row_size,)), dma((col_size,)), dma((col_size,)),
        ],
        compiler_params=pltpu.CompilerParams(
            collective_id=1, has_side_effects=True, vmem_limit_bytes=48 * 1024 * 1024
        ),
    )(row_signs, sampled, matrix, right_sides)


def local(matrix, row_signs, sampled_rows, right_sides):
    sampled = sampled_rows.reshape(lax.axis_size("rows"), -1)
    gram_matrix, first, norm = sketched_gram(row_signs.reshape(1, -1), sampled, matrix, right_sides)
    inverse = inverse_factor(gram_matrix)
    return lsqr(matrix, inverse, right_sides, first, norm)


def solution(mesh):
    in_specs = (P("rows", "cols"), P("rows"), P("rows", None), P(None, "rows"))
    out_specs = (P(None, "cols"), P(None, "rows"))
    return jax.shard_map(local, mesh=mesh, in_specs=in_specs, out_specs=out_specs, check_vma=False)
```
